128 devices in a mesh: rows: 64 (over x_lo, y, z, core), sub: 2 (over x_hi).
Axes of the slice: x: 4 (x_hi: 2, x_lo: 2; x = x_hi * 2 + x_lo), y: 4, z: 4, core: 2. Of those that a mesh axis runs over, the one named last changes fastest.
Arguments:
- vectors: bfloat16 [131072, 1024], P(('rows', 'sub')), may hold values from -10 to 10
- list_ids: int32 [131072], P(('rows', 'sub')), may hold values from 0 to 65535, as said below
- codes: int32 [131072, 64], P(('rows', 'sub')), may hold values from 0 to 255
- centroids: bfloat16 [65536, 1024], P(('rows', 'sub')), may hold values from -6 to 6
- codebooks: float32 [64, 16, 256], P('sub'), may hold values from -6 to 6
Outputs:
- new_centroids: float32 [65536, 1024], P(('rows', 'sub'))
- new_codebooks: float32 [64, 16, 256], P('sub')
- distortion: float32 [64, 256], P('sub')
The draws below stay inside these ranges and needn't reach their ends.
Inputs may be any that keep to these rules, and one draw needn't show every extreme that they name: `list_ids`: in each device's block of 1024 rows, the j-th run of 8 rows holds only ids from j * 512 to j * 512 + 511.
All inputs are finite; a program needn't handle non-finite values.
Results may differ from the reference program's by a relative error of at most 0.0003.
Values may be sent and summed in bfloat16 or wider, within the bound.
No kernel may reach another device: no remote copies, remote signals or barrier semaphores. Data moves between devices by JAX's collectives and lax.ppermute only.
A program may use at most 192 MiB of HBM per device.

```python
import math
import jax
import jax.numpy as jnp
from jax import lax

ROWS_DEV = 1024
LIST_DEV = 512
M = 64
DS = 16
K = 256
D = 1024
NVEC = 131072
LISTS = 65536
RUN = 8
PRIOR_LISTS = 2
PRIOR_CODES = 512
DEVICES = 128


def shared_codes(key):
    return jax.random.randint(jax.random.fold_in(key, 101), (NVEC, M), 0, K).astype(jnp.int32)


def draw_codes(key, part):
    return shared_codes(key)


def draw_vectors(key, part):
    chosen_codes = shared_codes(key)
    key = jax.random.fold_in(key, 7)
    table_key, noise_key = jax.random.split(key)
    table = 0.75 * jnp.clip(jax.random.normal(table_key, (M, K, DS), jnp.float32), -3.0, 3.0)
    noise = 0.25 * jnp.clip(jax.random.normal(noise_key, (NVEC, M, DS), jnp.float32), -4.0, 4.0)
    subspace_index = jnp.arange(M, dtype=jnp.int32)[None, :]
    picked = table[subspace_index, chosen_codes]
    positions = jnp.arange(NVEC, dtype=jnp.int32)
    owner = (positions % ROWS_DEV // RUN).astype(jnp.float32)
    factor = 1.0 + 2.0 * owner / max(DEVICES - 1, 1)
    return ((picked + noise) * factor[:, None, None]).reshape(NVEC, M * DS).astype(jnp.bfloat16)


def draw_list_ids(key, part):
    key = jax.random.fold_in(key, 13)
    positions = jnp.arange(NVEC, dtype=jnp.int32)
    owner = positions % ROWS_DEV // RUN
    within = jax.random.randint(key, (NVEC,), 0, LIST_DEV).astype(jnp.int32)
    return (owner * LIST_DEV + within).astype(jnp.int32)


def block_levels(stream_key, extent, shards, smallest, largest):
    gain, own = 1.0, jax.random.fold_in(stream_key, 6)
    for dim, blocks in shards:
        steps = jnp.exp(jax.random.uniform(jax.random.fold_in(own, dim), (blocks,), jnp.float32, smallest / len(shards), largest / len(shards)))
        gain = gain * jnp.repeat(steps, extent[dim] // blocks).reshape([-1 if axis == dim else 1 for axis in range(len(extent))])
    return gain


def gaussian(own_key, shape, scale, reach, cuts=(), held_as=jnp.bfloat16):
    result = scale * jax.random.normal(own_key, shape, jnp.float32)
    if cuts:
        result = result * block_levels(own_key, shape, cuts, -0.22, 0.18)
    return jnp.clip(result, -reach, reach).astype(held_as)


def setup_inputs(seed: int = 0) -> dict:
    key_list = jax.random.split(jax.random.key(seed), 6)
    return {
        "vectors": draw_vectors(jax.random.fold_in(key_list[5], 71), 0),
        "list_ids": draw_list_ids(jax.random.fold_in(key_list[5], 71), 0),
        "codes": draw_codes(jax.random.fold_in(key_list[5], 71), 0),
        "centroids": gaussian(key_list[3], (LISTS, D), 1.0, 6.0, ((0, 128),)),
        "codebooks": gaussian(key_list[4], (M, DS, K), 1.0, 6.0, ((0, 2),), jnp.float32),
    }


def reference(vectors, list_ids, codes, centroids, codebooks):
    block_rows = math.gcd(NVEC, 16384)
    blocks = NVEC // block_rows
    vector_blocks = vectors.reshape(blocks, block_rows, D)
    id_blocks = list_ids.reshape(blocks, block_rows)
    code_blocks = codes.reshape(blocks, block_rows, M)

    def coarse_step(running, pieces):
        totals, tallies = running
        portion, portion_ids = pieces
        totals = totals + jax.ops.segment_sum(portion.astype(jnp.float32), portion_ids, num_segments=LISTS)
        tallies = tallies + jax.ops.segment_sum(jnp.ones(portion_ids.shape, jnp.float32), portion_ids, num_segments=LISTS)
        return (totals, tallies), None

    start = (jnp.zeros((LISTS, D), jnp.float32), jnp.zeros((LISTS,), jnp.float32))
    (list_totals, list_counts), _unused = lax.scan(coarse_step, start, (vector_blocks, id_blocks))
    new_centroids = (list_totals + PRIOR_LISTS * centroids.astype(jnp.float32)) / (list_counts[:, None] + PRIOR_LISTS)
    offsets = jnp.arange(M, dtype=jnp.int32) * K

    def residual_of(portion, portion_ids):
        rounded = (portion.astype(jnp.float32) - new_centroids[portion_ids]).astype(jnp.bfloat16)
        rounded = lax.optimization_barrier(rounded)
        return rounded.astype(jnp.float32).reshape(-1, DS)

    def code_step(running, pieces):
        totals, tallies = running
        portion, portion_ids, portion_codes = pieces
        flat_rows = residual_of(portion, portion_ids)
        segment = (portion_codes + offsets[None, :]).astype(jnp.int32).reshape(-1)
        totals = totals + jax.ops.segment_sum(flat_rows, segment, num_segments=M * K)
        tallies = tallies + jax.ops.segment_sum(jnp.ones(segment.shape, jnp.float32), segment, num_segments=M * K)
        return (totals, tallies), None

    start = (jnp.zeros((M * K, DS), jnp.float32), jnp.zeros((M * K,), jnp.float32))
    (code_totals, code_counts), _unused = lax.scan(code_step, start, (vector_blocks, id_blocks, code_blocks))
    old_flat = jnp.transpose(codebooks, (0, 2, 1)).reshape(M * K, DS)
    new_flat = (code_totals + PRIOR_CODES * old_flat) / (code_counts[:, None] + PRIOR_CODES)

    def error_step(running, pieces):
        portion, portion_ids, portion_codes = pieces
        flat_rows = residual_of(portion, portion_ids)
        segment = (portion_codes + offsets[None, :]).astype(jnp.int32).reshape(-1)
        gap = flat_rows - new_flat[segment]
        return running + jax.ops.segment_sum(jnp.sum(gap * gap, axis=1), segment, num_segments=M * K), None

    errors, _unused = lax.scan(error_step, jnp.zeros((M * K,), jnp.float32), (vector_blocks, id_blocks, code_blocks))
    new_codebooks = jnp.transpose(new_flat.reshape(M, K, DS), (0, 2, 1))
    distortion = (errors / (code_counts + 1.0)).reshape(M, K)
    return new_centroids, new_codebooks, distortion
```

```python
import functools

import jax
import jax.numpy as jnp
from jax import lax
from jax.experimental import pallas as pl
from jax.experimental.pallas import tpu as pltpu
from jax.sharding import PartitionSpec as P

LANES = 128
COLS = 256


def split3(x):
    hi = x.astype(jnp.bfloat16)
    rest = x - hi.astype(jnp.float32)
    mid = rest.astype(jnp.bfloat16)
    lo = (rest - mid.astype(jnp.float32)).astype(jnp.bfloat16)
    return hi, mid, lo


def dot(a, b):
    return jnp.dot(a, b, preferred_element_type=jnp.float32)


def local_kernel(
    subs, width, prior_lists, v_ref, aux_ref, cent_ref, nc_ref, out_ref, hot, hot_t, cnt, code_t
):
    rows = v_ref.shape[0]
    lists = cent_ref.shape[0]
    levels = out_ref.shape[1] * LANES
    here = COLS // width
    step = pl.program_id(0)

    @pl.when(step == 0)
    def _():
        aux = aux_ref[...].astype(jnp.float32)
        aux_t = jnp.transpose(aux)
        row_ids = (aux_t[subs : subs + 1] * 256.0 + aux_t[subs + 1 : subs + 2]).astype(jnp.int32)
        col_ids = (aux[:, subs : subs + 1] * 256.0 + aux[:, subs + 1 : subs + 2]).astype(jnp.int32)
        level = lax.broadcasted_iota(jnp.int32, (lists, rows), 0)
        hot[...] = jnp.where(level == row_ids, 1.0, 0.0).astype(jnp.bfloat16)
        level = lax.broadcasted_iota(jnp.int32, (rows, lists), 1)
        hot_t[...] = jnp.where(level == col_ids, 1.0, 0.0).astype(jnp.bfloat16)
        cnt[...] = dot(hot[...], jnp.ones((rows, LANES), jnp.bfloat16))
        for block in range(subs // here):
            code_t[block] = aux_t[block * here : (block + 1) * here]

    v = v_ref[...]
    totals = dot(hot[...], v)
    counts = jnp.concatenate([cnt[...]] * (COLS // LANES), axis=1)
    nc = (totals + prior_lists * cent_ref[...].astype(jnp.float32)) / (counts + prior_lists)
    nc_ref[...] = nc
    hi, mid, lo = split3(nc)
    picked = (dot(hot_t[...], hi) + dot(hot_t[...], mid)) + dot(hot_t[...], lo)
    resid = (v.astype(jnp.float32) - picked).astype(jnp.bfloat16)

    wide = resid.astype(jnp.float32)
    square = wide * wide
    square_hi = square.astype(jnp.bfloat16)
    square_lo = (square - square_hi.astype(jnp.float32)).astype(jnp.bfloat16)
    source = lax.broadcasted_iota(jnp.int32, (COLS, LANES), 0) // width
    target = lax.broadcasted_iota(jnp.int32, (COLS, LANES), 1)
    spread = jnp.where((target % here == source) & (target < 3 * here), 1.0, 0.0).astype(
        jnp.bfloat16
    )
    norms = dot(square_hi, spread) + dot(square_lo, spread)
    n_hi, n_mid, n_lo = split3(norms)
    lane = lax.broadcasted_iota(jnp.int32, (rows, LANES), 1)
    extra = jnp.where(
        lane < here,
        n_hi.astype(jnp.float32),
        jnp.where(
            lane < 2 * here,
            n_mid.astype(jnp.float32),
            jnp.where(lane < 3 * here, n_lo.astype(jnp.float32), 1.0),
        ),
    ).astype(jnp.bfloat16)

    codes = code_t[step].astype(jnp.int32)
    level = lax.broadcasted_iota(jnp.int32, (levels, rows), 0)
    lane = lax.broadcasted_iota(jnp.int32, (levels, LANES), 1)
    group = LANES // width
    extra_sum = jnp.zeros((levels, LANES), jnp.float32)
    pieces = []
    for part in range(COLS // LANES):
        weights = jnp.concatenate(
            [resid[:, part * LANES : (part + 1) * LANES], extra], axis=1
        )
        sums = jnp.zeros((levels, LANES), jnp.float32)
        for k in range(group):
            i = part * group + k
            onehot = jnp.where(level == codes[i : i + 1], 1.0, 0.0).astype(jnp.bfloat16)
            found = dot(onehot, weights)
            sums = jnp.where(lane // width == k, found[:, :LANES], sums)
            extra_sum = jnp.where(lane % here == i, found[:, LANES:], extra_sum)
        pieces.append(jnp.transpose(sums))
    tail = jnp.transpose(extra_sum)
    norm_sum = (tail[:here] + tail[here : 2 * here]) + tail[2 * here : 3 * here]
    count_sum = tail[3 * here : 4 * here]
    blank = jnp.zeros((out_ref.shape[3] - width - 2, LANES), jnp.float32)
    for i in range(here):
        part, k = divmod(i, group)
        block = pieces[part][k * width : (k + 1) * width]
        for half in range(levels // LANES):
            at = slice(half * LANES, (half + 1) * LANES)
            out_ref[i, half, 0] = jnp.concatenate(
                [block[:, at], count_sum[i : i + 1, at], norm_sum[i : i + 1, at], blank], axis=0
            )


def local_pass(arrived, centroids, subs, width, levels, prior_lists, parts):
    rows = arrived.shape[0]
    lists, dims = centroids.shape
    here = COLS // width
    steps = dims // COLS
    per_part = steps // parts
    halves = levels // LANES
    held = 8 * (-(-(width + 2) // 8))
    return pl.pallas_call(
        functools.partial(local_kernel, subs, width, prior_lists),
        grid=(steps,),
        in_specs=[
            pl.BlockSpec((rows, COLS), lambda j: (0, j)),
            pl.BlockSpec((rows, LANES), lambda j: (0, dims // LANES)),
            pl.BlockSpec((lists, COLS), lambda j: (0, j)),
        ],
        out_specs=[
            pl.BlockSpec((lists, COLS), lambda j: (0, j)),
            pl.BlockSpec(
                (here, halves, 1, held, LANES),
                lambda j: (j % per_part, 0, j // per_part, 0, 0),
            ),
        ],
        out_shape=[
            jax.ShapeDtypeStruct((lists, dims), jnp.float32),
            jax.ShapeDtypeStruct((subs // parts, halves, parts, held, LANES), jnp.float32),
        ],
        scratch_shapes=[
            pltpu.VMEM((lists, rows), jnp.bfloat16),
            pltpu.VMEM((rows, lists), jnp.bfloat16),
            pltpu.VMEM((lists, LANES), jnp.float32),
            pltpu.VMEM((steps, here, rows), jnp.float32),
        ],
        compiler_params=pltpu.CompilerParams(vmem_limit_bytes=48 * 1024 * 1024),
        name="local_pass",
    )(arrived, arrived, centroids)


def owner_kernel(width, prior, part_ref, old_ref, out_ref):
    parts = part_ref[...]
    sums = parts[:, :width]
    counts = parts[:, width : width + 1]
    norms = parts[:, width + 1 : width + 2]
    total = jnp.sum(sums, axis=0)
    count = jnp.sum(counts, axis=0)
    new = (total + prior * old_ref[...]) / (count + prior)
    share = 1.0 / jnp.maximum(counts, 1.0)
    mean = sums * share
    gap = mean - new[None]
    inner = norms - jnp.sum(sums * mean, axis=1, keepdims=True)
    outer = counts * jnp.sum(gap * gap, axis=1, keepdims=True)
    errors = jnp.sum(jnp.maximum(inner, 0.0) + outer, axis=0)
    distortion = errors / (count + 1.0)
    blank = jnp.zeros((out_ref.shape[0] - width - 1, LANES), jnp.float32)
    out_ref[...] = jnp.concatenate([new, distortion, blank], axis=0)


def on_device(vectors, list_ids, codes, centroids, codebooks):
    rows, dims = vectors.shape
    owners = lax.axis_size("rows") * lax.axis_size("sub")
    lists = centroids.shape[0]
    subs = codes.shape[1]
    my_subs, width, levels = codebooks.shape
    halves = levels // LANES
    prior_lists = rows // lists
    prior_codes = rows * owners // levels
    local_ids = list_ids % lists
    aux = jnp.concatenate(
        [
            codes,
            (local_ids // 256)[:, None],
            (local_ids % 256)[:, None],
            jnp.zeros((rows, LANES - subs - 2), jnp.int32),
        ],
        axis=1,
    ).astype(jnp.bfloat16)
    sent = jnp.concatenate([vectors, aux], axis=1)
    arrived = lax.all_to_all(sent, ("rows", "sub"), split_axis=0, concat_axis=0, tiled=True)
    new_centroids, partials = local_pass(
        arrived, centroids, subs, width, levels, float(prior_lists), lax.axis_size("sub")
    )
    held = partials.shape[3]
    partials = partials.reshape(owners, held, LANES)
    mine = lax.all_to_all(partials, ("rows", "sub"), split_axis=0, concat_axis=0, tiled=True)
    place = lax.axis_index("rows")
    old = lax.dynamic_slice(
        codebooks, (place // halves, 0, (place % halves) * LANES), (1, width, LANES)
    )[0]
    done = pl.pallas_call(
        functools.partial(owner_kernel, width, float(prior_codes)),
        out_shape=jax.ShapeDtypeStruct((held, LANES), jnp.float32),
        compiler_params=pltpu.CompilerParams(vmem_limit_bytes=48 * 1024 * 1024),
        name="owner_pass",
    )(mine, old)
    copies = jnp.broadcast_to(done[None], (my_subs * halves, held, LANES))
    gathered = lax.all_to_all(copies, "rows", split_axis=0, concat_axis=0, tiled=True)
    gathered = gathered.reshape(my_subs, halves, held, LANES)
    table = jnp.transpose(gathered[:, :, :width], (0, 2, 1, 3)).reshape(my_subs, width, levels)
    distortion = gathered[:, :, width].reshape(my_subs, levels)
    return new_centroids, table, distortion


def solution(mesh):
    in_specs = (
        P(("rows", "sub"), None),
        P(("rows", "sub")),
        P(("rows", "sub"), None),
        P(("rows", "sub"), None),
        P("sub", None, None),
    )
    out_specs = (P(("rows", "sub"), None), P("sub", None, None), P("sub", None))
    return jax.shard_map(
        on_device, mesh=mesh, in_specs=in_specs, out_specs=out_specs, check_vma=False
    )
```

```python
import functools

import jax
import jax.numpy as jnp
from jax import lax
from jax.experimental import pallas as pl
from jax.experimental.pallas import tpu as pltpu
from jax.sharding import Mesh, PartitionSpec as P

LANES = 128
COLS = 256
CORES = 2
MIB = 1024 * 1024
IN_VMEM = pl.BlockSpec(memory_space=pltpu.VMEM)
SPLIT = ("chip", "core", "sub")


def split3(x):
    hi = x.astype(jnp.bfloat16)
    rest = x - hi.astype(jnp.float32)
    mid = rest.astype(jnp.bfloat16)
    lo = (rest - mid.astype(jnp.float32)).astype(jnp.bfloat16)
    return hi, mid, lo


def dot(a, b):
    return jnp.dot(a, b, preferred_element_type=jnp.float32)


def pack_kernel(lists, v_ref, ids_ref, codes_ref, out_ref, sem):
    rows, dims = v_ref.shape
    subs = codes_ref.shape[0]
    copy = pltpu.make_async_copy(v_ref, out_ref.at[:, :dims], sem)
    copy.start()
    ids = lax.rem(ids_ref[...], lists)
    high = lax.div(ids, 256)
    aux = jnp.concatenate(
        [
            codes_ref[...].astype(jnp.float32),
            high.astype(jnp.float32),
            (ids - 256 * high).astype(jnp.float32),
            jnp.zeros((LANES - subs - 2, rows), jnp.float32),
        ],
        axis=0,
    )
    out_ref[:, dims:] = jnp.transpose(aux).astype(jnp.bfloat16)
    copy.wait()


def pack(vectors, list_ids, codes, lists):
    rows, dims = vectors.shape
    return pl.pallas_call(
        functools.partial(pack_kernel, lists),
        in_specs=[pl.BlockSpec(memory_space=pl.ANY), IN_VMEM, IN_VMEM],
        out_specs=IN_VMEM,
        out_shape=jax.ShapeDtypeStruct((rows, dims + LANES), jnp.bfloat16),
        scratch_shapes=[pltpu.SemaphoreType.DMA],
        compiler_params=pltpu.CompilerParams(vmem_limit_bytes=12 * MIB),
        name="pack",
    )(vectors, list_ids.reshape(1, rows), jnp.transpose(codes))


def local_kernel(
    subs,
    width,
    parts,
    prior,
    chunk,
    core_ref,
    arr_ref,
    cent_ref,
    nc_ref,
    keep_ref,
    give_ref,
    hot,
    inv,
    code_t,
    table,
    picked,
    resid,
    extra,
    ids_v,
    ids_s,
    sem,
):
    rows = arr_ref.shape[0]
    lists, dims = cent_ref.shape
    levels = 2 * LANES
    here = COLS // width
    group = LANES // width
    tiles = dims // LANES
    side = COLS // LANES
    held = width + 2
    first_core = core_ref[0] == 0

    aux = arr_ref[:, dims:].astype(jnp.float32)
    aux_t = jnp.transpose(aux)
    row_ids = (aux_t[subs : subs + 1] * 256.0 + aux_t[subs + 1 : subs + 2]).astype(jnp.int32)
    ids_v[...] = row_ids * tiles
    copy = pltpu.make_async_copy(ids_v, ids_s, sem)
    copy.start()
    level = lax.broadcasted_iota(jnp.int32, (lists, rows), 0)
    hot[...] = jnp.where(level == row_ids, 1.0, 0.0).astype(jnp.bfloat16)
    counts = dot(hot[...], jnp.ones((rows, LANES), jnp.bfloat16))
    inv[...] = 1.0 / (counts + prior)
    for b in range(subs // here):
        code_t[b] = aux_t[b * here : (b + 1) * here].astype(jnp.int32)

    for j in range(dims // COLS):
        totals = dot(hot[...], arr_ref[:, j * COLS : (j + 1) * COLS])
        for h in range(side):
            tile = j * side + h
            at = slice(tile * LANES, (tile + 1) * LANES)
            old = cent_ref[:, at].astype(jnp.float32)
            nc = (totals[:, h * LANES : (h + 1) * LANES] + prior * old) * inv[...]
            nc_ref[:, at] = nc
            table[pl.ds(tile, lists, stride=tiles), :] = nc
    copy.wait()

    def pick(q, _):
        for u in range(8):
            r = q * 8 + u
            row = table[pl.ds(pl.multiple_of(ids_s[0, r], 8), tiles), :]
            picked[pl.ds(pl.multiple_of(r * tiles, 8), tiles), :] = row
        return 0

    lax.fori_loop(0, rows // 8, pick, 0)

    source = lax.broadcasted_iota(jnp.int32, (COLS, LANES), 0) // width
    target = lax.broadcasted_iota(jnp.int32, (COLS, LANES), 1)
    spread = jnp.where((target % here == source) & (target < 3 * here), 1.0, 0.0).astype(
        jnp.bfloat16
    )

    def columns(j, _):
        at = pl.ds(pl.multiple_of(j * COLS, COLS), COLS)
        for i in range(rows // chunk):
            ra = slice(i * chunk, (i + 1) * chunk)
            near = jnp.concatenate(
                [
                    picked[pl.ds(i * chunk * tiles + j * side + h, chunk, stride=tiles), :]
                    for h in range(side)
                ],
                axis=1,
            )
            r = (arr_ref[ra, at].astype(jnp.float32) - near).astype(jnp.bfloat16)
            resid[ra, :] = r
            wide = r.astype(jnp.float32)
            square = wide * wide
            square_hi = square.astype(jnp.bfloat16)
            square_lo = (square - square_hi.astype(jnp.float32)).astype(jnp.bfloat16)
            n_hi, n_mid, n_lo = split3(dot(square_hi, spread) + dot(square_lo, spread))
            lane = lax.broadcasted_iota(jnp.int32, (chunk, LANES), 1)
            extra[ra, :] = jnp.where(
                lane < here,
                n_hi.astype(jnp.float32),
                jnp.where(
                    lane < 2 * here,
                    n_mid.astype(jnp.float32),
                    jnp.where(lane < 3 * here, n_lo.astype(jnp.float32), 1.0),
                ),
            ).astype(jnp.bfloat16)

        codes = code_t[j]
        level = lax.broadcasted_iota(jnp.int32, (levels, rows), 0)
        lane = lax.broadcasted_iota(jnp.int32, (levels, LANES), 1)
        extra_sum = jnp.zeros((levels, LANES), jnp.float32)
        pieces = []
        for part in range(side):
            weights = jnp.concatenate(
                [resid[:, part * LANES : (part + 1) * LANES], extra[...]], axis=1
            )
            sums = jnp.zeros((levels, LANES), jnp.float32)
            for k in range(group):
                i = part * group + k
                onehot = jnp.where(level == codes[i : i + 1], 1.0, 0.0).astype(jnp.bfloat16)
                found = dot(onehot, weights)
                sums = jnp.where(lane // width == k, found[:, :LANES], sums)
                extra_sum = jnp.where(lane % here == i, found[:, LANES:], extra_sum)
            pieces.append(jnp.transpose(sums))
        tail = jnp.transpose(extra_sum)
        norm_sum = (tail[:here] + tail[here : 2 * here]) + tail[2 * here : 3 * here]
        count_sum = tail[3 * here : 4 * here]
        steps = subs // parts // here
        for i in range(here):
            part, k = divmod(i, group)
            block = jnp.concatenate(
                [
                    pieces[part][k * width : (k + 1) * width],
                    count_sum[i : i + 1],
                    norm_sum[i : i + 1],
                ],
                axis=0,
            )
            left, right = block[:, :LANES], block[:, LANES:]
            at_row = ((lax.rem(j, steps) * here + i) * parts + lax.div(j, steps)) * held
            keep_ref[pl.ds(at_row, held), :] = jnp.where(first_core, left, right)
            give_ref[pl.ds(at_row, held), :] = jnp.where(first_core, right, left)
        return 0

    lax.fori_loop(0, dims // COLS, columns, 0)


def local_pass(core, arrived, centroids, subs, width, prior, parts):
    rows = arrived.shape[0]
    lists, dims = centroids.shape
    tiles = dims // LANES
    here = COLS // width
    sums = jax.ShapeDtypeStruct((subs * (width + 2), LANES), jnp.float32)
    return pl.pallas_call(
        functools.partial(local_kernel, subs, width, parts, prior, 256),
        in_specs=[pl.BlockSpec(memory_space=pltpu.SMEM), IN_VMEM, IN_VMEM],
        out_specs=[IN_VMEM, IN_VMEM, IN_VMEM],
        out_shape=[jax.ShapeDtypeStruct((lists, dims), jnp.float32), sums, sums],
        scratch_shapes=[
            pltpu.VMEM((lists, rows), jnp.bfloat16),
            pltpu.VMEM((lists, LANES), jnp.float32),
            pltpu.VMEM((subs // here, here, rows), jnp.int32),
            pltpu.VMEM((lists * tiles, LANES), jnp.float32),
            pltpu.VMEM((rows * tiles, LANES), jnp.float32),
            pltpu.VMEM((rows, COLS), jnp.bfloat16),
            pltpu.VMEM((rows, LANES), jnp.bfloat16),
            pltpu.VMEM((1, rows), jnp.int32),
            pltpu.SMEM((1, rows), jnp.int32),
            pltpu.SemaphoreType.DMA,
        ],
        compiler_params=pltpu.CompilerParams(vmem_limit_bytes=32 * MIB),
        name="local_pass",
    )(core, arrived, centroids)


def owner_kernel(width, prior, copies, part_ref, old_ref, out_ref):
    held = width + 2
    sources = part_ref.shape[0] // held
    taken = [part_ref[pl.ds(i, sources, stride=held), :] for i in range(held)]
    sums, counts, norms = taken[:width], taken[width], taken[width + 1]
    count = jnp.sum(counts, axis=0, keepdims=True)
    share = 1.0 / jnp.maximum(counts, 1.0)
    inner = norms
    outer = jnp.zeros_like(norms)
    rows = []
    for d in range(width):
        total = jnp.sum(sums[d], axis=0, keepdims=True)
        new = (total + prior * old_ref[d : d + 1]) / (count + prior)
        mean = sums[d] * share
        gap = mean - new
        inner = inner - sums[d] * mean
        outer = outer + gap * gap
        rows.append(new)
    errors = jnp.sum(jnp.maximum(inner, 0.0) + counts * outer, axis=0, keepdims=True)
    rows.append(errors / (count + 1.0))
    result = jnp.concatenate(rows, axis=0)
    for c in range(copies):
        out_ref[c * (width + 1) : (c + 1) * (width + 1)] = result


def finish_kernel(width, core_ref, mine_ref, other_ref, table_ref, dist_ref):
    held = width + 1
    subs = table_ref.shape[0]
    first_core = core_ref[0] == 0
    for ref, at in ((0, slice(0, LANES)), (1, slice(LANES, 2 * LANES))):
        own = first_core if ref == 0 else jnp.logical_not(first_core)
        for m in range(subs):
            rows = slice(m * held, m * held + width)
            table_ref[m, :, at] = jnp.where(own, mine_ref[rows], other_ref[rows])
        last = pl.ds(width, subs, stride=held)
        dist_ref[:, at] = jnp.where(own, mine_ref[last, :], other_ref[last, :])


def on_device(vectors, list_ids, codes, centroids, codebooks):
    rows, dims = vectors.shape
    chips = lax.axis_size("chip")
    parts = lax.axis_size("sub")
    owners = chips * CORES * parts
    lists = centroids.shape[0]
    subs = codes.shape[1]
    my_subs, width, levels = codebooks.shape
    prior_lists = float(rows // lists)
    prior_codes = float(rows * owners // levels)
    core = lax.axis_index("core")
    core_arg = core.astype(jnp.int32).reshape(1)
    swap = [(0, 1), (1, 0)]

    sent = pack(vectors, list_ids, codes, lists)
    arrived = lax.all_to_all(sent, SPLIT, split_axis=0, concat_axis=0, tiled=True)
    new_centroids, keep, give = local_pass(
        core_arg, arrived, centroids, subs, width, prior_lists, parts
    )
    paired = keep + lax.ppermute(give, "core", swap)
    held = width + 2
    mine = lax.all_to_all(
        paired.reshape(chips * parts, 1, held * LANES),
        ("chip", "sub"),
        split_axis=0,
        concat_axis=0,
        tiled=True,
    ).reshape(chips * parts * held, LANES)
    old = lax.dynamic_slice(
        codebooks, (lax.axis_index("chip"), 0, core * LANES), (1, width, LANES)
    )[0]
    held = width + 1
    done = pl.pallas_call(
        functools.partial(owner_kernel, width, prior_codes, chips),
        in_specs=[IN_VMEM, IN_VMEM],
        out_specs=IN_VMEM,
        out_shape=jax.ShapeDtypeStruct((chips * held, LANES), jnp.float32),
        compiler_params=pltpu.CompilerParams(vmem_limit_bytes=8 * MIB),
        name="owner_pass",
    )(mine, old)
    half = lax.all_to_all(
        done.reshape(chips, 1, held * LANES), "chip", split_axis=0, concat_axis=0, tiled=True
    ).reshape(chips * held, LANES)
    other = lax.ppermute(half, "core", swap)
    table, distortion = pl.pallas_call(
        functools.partial(finish_kernel, width),
        in_specs=[pl.BlockSpec(memory_space=pltpu.SMEM), IN_VMEM, IN_VMEM],
        out_specs=[IN_VMEM, IN_VMEM],
        out_shape=[
            jax.ShapeDtypeStruct((my_subs, width, levels), jnp.float32),
            jax.ShapeDtypeStruct((my_subs, levels), jnp.float32),
        ],
        compiler_params=pltpu.CompilerParams(vmem_limit_bytes=8 * MIB),
        name="finish",
    )(core_arg, half, other)
    return new_centroids, table, distortion


def solution(mesh):
    parts = mesh.shape["sub"]
    cores = Mesh(mesh.devices.reshape(-1, CORES, parts), SPLIT)
    in_specs = (
        P(SPLIT, None),
        P(SPLIT),
        P(SPLIT, None),
        P(SPLIT, None),
        P("sub", None, None),
    )
    out_specs = (P(SPLIT, None), P("sub", None, None), P("sub", None))
    return jax.shard_map(
        on_device, mesh=cores, in_specs=in_specs, out_specs=out_specs, check_vma=False
    )
```

```python
import functools

import jax
import jax.numpy as jnp
from jax import lax
from jax.experimental import pallas as pl
from jax.experimental.pallas import tpu as pltpu
from jax.sharding import Mesh, PartitionSpec as P

LANES = 128
COLS = 256
CORES = 2
MIB = 1024 * 1024
IN_VMEM = pl.BlockSpec(memory_space=pltpu.VMEM)
SPLIT = ("chip", "core", "sub")


def split3(x):
    hi = x.astype(jnp.bfloat16)
    rest = x - hi.astype(jnp.float32)
    mid = rest.astype(jnp.bfloat16)
    lo = (rest - mid.astype(jnp.float32)).astype(jnp.bfloat16)
    return hi, mid, lo


def dot(a, b):
    return jnp.dot(a, b, preferred_element_type=jnp.float32)


def pack_kernel(lists, v_ref, ids_ref, codes_ref, out_ref, ids_v, codes_v, aux_v, sems):
    rows, dims = v_ref.shape
    subs = codes_ref.shape[0]
    moves = [
        pltpu.make_async_copy(codes_ref, codes_v, sems.at[0]),
        pltpu.make_async_copy(ids_ref, ids_v, sems.at[1]),
        pltpu.make_async_copy(v_ref, out_ref.at[:, :dims], sems.at[2]),
    ]
    for move in moves:
        move.start()
    moves[0].wait()
    moves[1].wait()
    ids = lax.rem(ids_v[...], lists)
    high = lax.div(ids, 256)
    aux = jnp.concatenate(
        [
            codes_v[...].astype(jnp.float32),
            high.astype(jnp.float32),
            (ids - 256 * high).astype(jnp.float32),
            jnp.zeros((LANES - subs - 2, rows), jnp.float32),
        ],
        axis=0,
    )
    aux_v[...] = jnp.transpose(aux).astype(jnp.bfloat16)
    last = pltpu.make_async_copy(aux_v, out_ref.at[:, dims:], sems.at[3])
    last.start()
    moves[2].wait()
    last.wait()


def pack(vectors, list_ids, codes, lists):
    rows, dims = vectors.shape
    subs = codes.shape[1]
    anywhere = pl.BlockSpec(memory_space=pl.ANY)
    return pl.pallas_call(
        functools.partial(pack_kernel, lists),
        in_specs=[anywhere, anywhere, anywhere],
        out_specs=anywhere,
        out_shape=jax.ShapeDtypeStruct((rows, dims + LANES), jnp.bfloat16),
        scratch_shapes=[
            pltpu.VMEM((1, rows), jnp.int32),
            pltpu.VMEM((subs, rows), jnp.int32),
            pltpu.VMEM((rows, LANES), jnp.bfloat16),
            pltpu.SemaphoreType.DMA((4,)),
        ],
        compiler_params=pltpu.CompilerParams(vmem_limit_bytes=56 * MIB),
        name="pack",
    )(vectors, list_ids.reshape(1, rows), jnp.transpose(codes))


def local_kernel(
    subs,
    width,
    parts,
    prior,
    chunk,
    core_ref,
    arr_ref,
    cent_ref,
    nc_ref,
    keep_ref,
    give_ref,
    hot,
    inv,
    code_t,
    table,
    picked,
    resid,
    extra,
    ids_v,
    ids_s,
    nc_v,
    sem,
    nc_sem,
):
    rows = arr_ref.shape[0]
    lists, dims = cent_ref.shape
    levels = 2 * LANES
    here = COLS // width
    group = LANES // width
    tiles = dims // LANES
    side = COLS // LANES
    held = width + 2
    first_core = core_ref[0] == 0

    aux = arr_ref[:, dims:].astype(jnp.float32)
    aux_t = jnp.transpose(aux)
    row_ids = (aux_t[subs : subs + 1] * 256.0 + aux_t[subs + 1 : subs + 2]).astype(jnp.int32)
    ids_v[...] = row_ids * tiles
    copy = pltpu.make_async_copy(ids_v, ids_s, sem)
    copy.start()
    level = lax.broadcasted_iota(jnp.int32, (lists, rows), 0)
    hot[...] = jnp.where(level == row_ids, 1.0, 0.0).astype(jnp.bfloat16)
    counts = dot(hot[...], jnp.ones((rows, LANES), jnp.bfloat16))
    inv[...] = 1.0 / (counts + prior)
    for b in range(subs // here):
        code_t[b] = aux_t[b * here : (b + 1) * here].astype(jnp.int32)

    for j in range(dims // COLS):
        totals = dot(hot[...], arr_ref[:, j * COLS : (j + 1) * COLS])
        for h in range(side):
            tile = j * side + h
            at = slice(tile * LANES, (tile + 1) * LANES)
            old = cent_ref[:, at].astype(jnp.float32)
            nc = (totals[:, h * LANES : (h + 1) * LANES] + prior * old) * inv[...]
            nc_v[:, at] = nc
            table[pl.ds(tile, lists, stride=tiles), :] = nc
    nc_copy = pltpu.make_async_copy(nc_v, nc_ref, nc_sem)
    nc_copy.start()
    copy.wait()

    def pick(q, _):
        for u in range(8):
            r = q * 8 + u
            row = table[pl.ds(pl.multiple_of(ids_s[0, r], 8), tiles), :]
            picked[pl.ds(pl.multiple_of(r * tiles, 8), tiles), :] = row
        return 0

    lax.fori_loop(0, rows // 8, pick, 0)

    source = lax.broadcasted_iota(jnp.int32, (COLS, LANES), 0) // width
    target = lax.broadcasted_iota(jnp.int32, (COLS, LANES), 1)
    spread = jnp.where((target % here == source) & (target < 3 * here), 1.0, 0.0).astype(
        jnp.bfloat16
    )

    def columns(j, _):
        at = pl.ds(pl.multiple_of(j * COLS, COLS), COLS)
        for i in range(rows // chunk):
            ra = slice(i * chunk, (i + 1) * chunk)
            near = jnp.concatenate(
                [
                    picked[pl.ds(i * chunk * tiles + j * side + h, chunk, stride=tiles), :]
                    for h in range(side)
                ],
                axis=1,
            )
            r = (arr_ref[ra, at].astype(jnp.float32) - near).astype(jnp.bfloat16)
            resid[ra, :] = r
            wide = r.astype(jnp.float32)
            square = wide * wide
            square_hi = square.astype(jnp.bfloat16)
            square_lo = (square - square_hi.astype(jnp.float32)).astype(jnp.bfloat16)
            n_hi, n_mid, n_lo = split3(dot(square_hi, spread) + dot(square_lo, spread))
            lane = lax.broadcasted_iota(jnp.int32, (chunk, LANES), 1)
            extra[ra, :] = jnp.where(
                lane < here,
                n_hi.astype(jnp.float32),
                jnp.where(
                    lane < 2 * here,
                    n_mid.astype(jnp.float32),
                    jnp.where(lane < 3 * here, n_lo.astype(jnp.float32), 1.0),
                ),
            ).astype(jnp.bfloat16)

        codes = code_t[j]
        level = lax.broadcasted_iota(jnp.int32, (levels, rows), 0)
        lane = lax.broadcasted_iota(jnp.int32, (levels, LANES), 1)
        extra_sum = jnp.zeros((levels, LANES), jnp.float32)
        pieces = []
        for part in range(side):
            weights = jnp.concatenate(
                [resid[:, part * LANES : (part + 1) * LANES], extra[...]], axis=1
            )
            sums = jnp.zeros((levels, LANES), jnp.float32)
            for k in range(group):
                i = part * group + k
                onehot = jnp.where(level == codes[i : i + 1], 1.0, 0.0).astype(jnp.bfloat16)
                found = dot(onehot, weights)
                sums = jnp.where(lane // width == k, found[:, :LANES], sums)
                extra_sum = jnp.where(lane % here == i, found[:, LANES:], extra_sum)
            pieces.append(jnp.transpose(sums))
        tail = jnp.transpose(extra_sum)
        norm_sum = (tail[:here] + tail[here : 2 * here]) + tail[2 * here : 3 * here]
        count_sum = tail[3 * here : 4 * here]
        steps = subs // parts // here
        for i in range(here):
            part, k = divmod(i, group)
            block = jnp.concatenate(
                [
                    pieces[part][k * width : (k + 1) * width],
                    count_sum[i : i + 1],
                    norm_sum[i : i + 1],
                ],
                axis=0,
            )
            left, right = block[:, :LANES], block[:, LANES:]
            at_row = ((lax.rem(j, steps) * here + i) * parts + lax.div(j, steps)) * held
            keep_ref[pl.ds(at_row, held), :] = jnp.where(first_core, left, right)
            give_ref[pl.ds(at_row, held), :] = jnp.where(first_core, right, left)
        return 0

    lax.fori_loop(0, dims // COLS, columns, 0)
    nc_copy.wait()


def local_pass(core, arrived, centroids, subs, width, prior, parts):
    rows = arrived.shape[0]
    lists, dims = centroids.shape
    tiles = dims // LANES
    here = COLS // width
    sums = jax.ShapeDtypeStruct((subs * (width + 2), LANES), jnp.float32)
    return pl.pallas_call(
        functools.partial(local_kernel, subs, width, parts, prior, 256),
        in_specs=[pl.BlockSpec(memory_space=pltpu.SMEM), IN_VMEM, IN_VMEM],
        out_specs=[pl.BlockSpec(memory_space=pl.ANY), IN_VMEM, IN_VMEM],
        out_shape=[jax.ShapeDtypeStruct((lists, dims), jnp.float32), sums, sums],
        scratch_shapes=[
            pltpu.VMEM((lists, rows), jnp.bfloat16),
            pltpu.VMEM((lists, LANES), jnp.float32),
            pltpu.VMEM((subs // here, here, rows), jnp.int32),
            pltpu.VMEM((lists * tiles, LANES), jnp.float32),
            pltpu.VMEM((rows * tiles, LANES), jnp.float32),
            pltpu.VMEM((rows, COLS), jnp.bfloat16),
            pltpu.VMEM((rows, LANES), jnp.bfloat16),
            pltpu.VMEM((1, rows), jnp.int32),
            pltpu.SMEM((1, rows), jnp.int32),
            pltpu.VMEM((lists, dims), jnp.float32),
            pltpu.SemaphoreType.DMA,
            pltpu.SemaphoreType.DMA,
        ],
        compiler_params=pltpu.CompilerParams(vmem_limit_bytes=32 * MIB),
        name="local_pass",
    )(core, arrived, centroids)


def owner_kernel(width, prior, copies, part_ref, old_ref, out_ref):
    held = width + 2
    sources = part_ref.shape[0] // held
    taken = [part_ref[pl.ds(i, sources, stride=held), :] for i in range(held)]
    sums, counts, norms = taken[:width], taken[width], taken[width + 1]
    count = jnp.sum(counts, axis=0, keepdims=True)
    share = 1.0 / jnp.maximum(counts, 1.0)
    inner = norms
    outer = jnp.zeros_like(norms)
    rows = []
    for d in range(width):
        total = jnp.sum(sums[d], axis=0, keepdims=True)
        new = (total + prior * old_ref[d : d + 1]) / (count + prior)
        mean = sums[d] * share
        gap = mean - new
        inner = inner - sums[d] * mean
        outer = outer + gap * gap
        rows.append(new)
    errors = jnp.sum(jnp.maximum(inner, 0.0) + counts * outer, axis=0, keepdims=True)
    rows.append(errors / (count + 1.0))
    result = jnp.concatenate(rows, axis=0)
    for c in range(copies):
        out_ref[c * (width + 1) : (c + 1) * (width + 1)] = result


def finish_kernel(width, core_ref, mine_ref, other_ref, table_ref, dist_ref):
    held = width + 1
    subs = table_ref.shape[0]
    first_core = core_ref[0] == 0
    for ref, at in ((0, slice(0, LANES)), (1, slice(LANES, 2 * LANES))):
        own = first_core if ref == 0 else jnp.logical_not(first_core)
        for m in range(subs):
            rows = slice(m * held, m * held + width)
            table_ref[m, :, at] = jnp.where(own, mine_ref[rows], other_ref[rows])
        last = pl.ds(width, subs, stride=held)
        dist_ref[:, at] = jnp.where(own, mine_ref[last, :], other_ref[last, :])


def on_device(vectors, list_ids, codes, centroids, codebooks):
    rows, dims = vectors.shape
    chips = lax.axis_size("chip")
    parts = lax.axis_size("sub")
    owners = chips * CORES * parts
    lists = centroids.shape[0]
    subs = codes.shape[1]
    my_subs, width, levels = codebooks.shape
    prior_lists = float(rows // lists)
    prior_codes = float(rows * owners // levels)
    core = lax.axis_index("core")
    core_arg = core.astype(jnp.int32).reshape(1)
    swap = [(0, 1), (1, 0)]

    sent = pack(vectors, list_ids, codes, lists)
    arrived = lax.all_to_all(sent, SPLIT, split_axis=0, concat_axis=0, tiled=True)
    new_centroids, keep, give = local_pass(
        core_arg, arrived, centroids, subs, width, prior_lists, parts
    )
    paired = keep + lax.ppermute(give, "core", swap)
    held = width + 2
    mine = lax.all_to_all(
        paired.reshape(chips * parts, 1, held * LANES),
        ("chip", "sub"),
        split_axis=0,
        concat_axis=0,
        tiled=True,
    ).reshape(chips * parts * held, LANES)
    old = lax.dynamic_slice(
        codebooks, (lax.axis_index("chip"), 0, core * LANES), (1, width, LANES)
    )[0]
    held = width + 1
    done = pl.pallas_call(
        functools.partial(owner_kernel, width, prior_codes, chips),
        in_specs=[IN_VMEM, IN_VMEM],
        out_specs=IN_VMEM,
        out_shape=jax.ShapeDtypeStruct((chips * held, LANES), jnp.float32),
        compiler_params=pltpu.CompilerParams(vmem_limit_bytes=8 * MIB),
        name="owner_pass",
    )(mine, old)
    half = lax.all_to_all(
        done.reshape(chips, 1, held * LANES), "chip", split_axis=0, concat_axis=0, tiled=True
    ).reshape(chips * held, LANES)
    other = lax.ppermute(half, "core", swap)
    table, distortion = pl.pallas_call(
        functools.partial(finish_kernel, width),
        in_specs=[pl.BlockSpec(memory_space=pltpu.SMEM), IN_VMEM, IN_VMEM],
        out_specs=[IN_VMEM, IN_VMEM],
        out_shape=[
            jax.ShapeDtypeStruct((my_subs, width, levels), jnp.float32),
            jax.ShapeDtypeStruct((my_subs, levels), jnp.float32),
        ],
        compiler_params=pltpu.CompilerParams(vmem_limit_bytes=8 * MIB),
        name="finish",
    )(core_arg, half, other)
    return new_centroids, table, distortion


def solution(mesh):
    parts = mesh.shape["sub"]
    cores = Mesh(mesh.devices.reshape(-1, CORES, parts), SPLIT)
    in_specs = (
        P(SPLIT, None),
        P(SPLIT),
        P(SPLIT, None),
        P(SPLIT, None),
        P("sub", None, None),
    )
    out_specs = (P(SPLIT, None), P("sub", None, None), P("sub", None))
    return jax.shard_map(
        on_device, mesh=cores, in_specs=in_specs, out_specs=out_specs, check_vma=False
    )
```

```python
import functools

import jax
import jax.numpy as jnp
from jax import lax
from jax.experimental import pallas as pl
from jax.experimental.pallas import tpu as pltpu
from jax.sharding import Mesh, PartitionSpec as P

LANES = 128
COLS = 256
CORES = 2
MIB = 1024 * 1024
IN_VMEM = pl.BlockSpec(memory_space=pltpu.VMEM)
SPLIT = ("chip", "core", "sub")


def split3(x):
    hi = x.astype(jnp.bfloat16)
    rest = x - hi.astype(jnp.float32)
    mid = rest.astype(jnp.bfloat16)
    lo = (rest - mid.astype(jnp.float32)).astype(jnp.bfloat16)
    return hi, mid, lo


def dot(a, b):
    return jnp.dot(a, b, preferred_element_type=jnp.float32)


def pack_kernel(
    lists, pieces, v_ref, ids_ref, codes_ref, out_ref, held, ids_v, codes_v, ins, outs
):
    rows, dims = v_ref.shape
    subs = codes_ref.shape[0]
    step = rows // pieces
    first = [
        pltpu.make_async_copy(codes_ref, codes_v, ins.at[pieces]),
        pltpu.make_async_copy(ids_ref, ids_v, ins.at[pieces + 1]),
    ]
    moves = [
        pltpu.make_async_copy(
            v_ref.at[pl.ds(i * step, step)],
            held.at[pl.ds(i * step, step), pl.ds(0, dims)],
            ins.at[i],
        )
        for i in range(pieces)
    ]
    for move in first + moves:
        move.start()
    for move in first:
        move.wait()
    ids = lax.rem(ids_v[...], lists)
    high = lax.div(ids, 256)
    aux = jnp.concatenate(
        [
            codes_v[...].astype(jnp.float32),
            high.astype(jnp.float32),
            (ids - 256 * high).astype(jnp.float32),
            jnp.zeros((LANES - subs - 2, rows), jnp.float32),
        ],
        axis=0,
    )
    held[:, dims:] = jnp.transpose(aux).astype(jnp.bfloat16)
    sends = []
    for i, move in enumerate(moves):
        move.wait()
        at = pl.ds(i * step, step)
        send = pltpu.make_async_copy(held.at[at], out_ref.at[at], outs.at[i])
        send.start()
        sends.append(send)
    for send in sends:
        send.wait()


def pack(vectors, list_ids, codes, lists):
    rows, dims = vectors.shape
    subs = codes.shape[1]
    pieces = 8
    anywhere = pl.BlockSpec(memory_space=pl.ANY)
    return pl.pallas_call(
        functools.partial(pack_kernel, lists, pieces),
        in_specs=[anywhere] * 3,
        out_specs=anywhere,
        out_shape=jax.ShapeDtypeStruct((rows, dims + LANES), jnp.bfloat16),
        scratch_shapes=[
            pltpu.VMEM((rows, dims + LANES), jnp.bfloat16),
            pltpu.VMEM((1, rows), jnp.int32),
            pltpu.VMEM((subs, rows), jnp.int32),
            pltpu.SemaphoreType.DMA((pieces + 2,)),
            pltpu.SemaphoreType.DMA((pieces,)),
        ],
        compiler_params=pltpu.CompilerParams(vmem_limit_bytes=58 * MIB),
        name="pack",
    )(vectors, list_ids.reshape(1, rows), jnp.transpose(codes))


def local_kernel(
    subs,
    width,
    parts,
    prior,
    chunk,
    core_ref,
    arr_ref,
    cent_ref,
    nc_ref,
    keep_ref,
    give_ref,
    hot,
    inv,
    code_t,
    table,
    picked,
    resid,
    extra,
    ids_v,
    ids_s,
    nc_v,
    sem,
    nc_sem,
):
    rows = arr_ref.shape[0]
    lists, dims = cent_ref.shape
    levels = 2 * LANES
    here = COLS // width
    group = LANES // width
    tiles = dims // LANES
    side = COLS // LANES
    held = width + 2
    first_core = core_ref[0] == 0

    aux = arr_ref[:, dims:].astype(jnp.float32)
    aux_t = jnp.transpose(aux)
    row_ids = (aux_t[subs : subs + 1] * 256.0 + aux_t[subs + 1 : subs + 2]).astype(jnp.int32)
    ids_v[...] = row_ids * tiles
    copy = pltpu.make_async_copy(ids_v, ids_s, sem)
    copy.start()
    level = lax.broadcasted_iota(jnp.int32, (lists, rows), 0)
    hot[...] = jnp.where(level == row_ids, 1.0, 0.0).astype(jnp.bfloat16)
    counts = dot(hot[...], jnp.ones((rows, LANES), jnp.bfloat16))
    inv[...] = 1.0 / (counts + prior)
    for b in range(subs // here):
        code_t[b] = aux_t[b * here : (b + 1) * here].astype(jnp.int32)

    for j in range(dims // COLS):
        totals = dot(hot[...], arr_ref[:, j * COLS : (j + 1) * COLS])
        for h in range(side):
            tile = j * side + h
            at = slice(tile * LANES, (tile + 1) * LANES)
            old = prior * cent_ref[:, at].astype(jnp.float32)
            nc = (totals[:, h * LANES : (h + 1) * LANES] + old) * inv[...]
            nc_v[:, at] = nc
            table[pl.ds(tile, lists, stride=tiles), :] = nc
    nc_copy = pltpu.make_async_copy(nc_v, nc_ref, nc_sem)
    nc_copy.start()
    copy.wait()

    def pick(q, _):
        for u in range(8):
            r = q * 8 + u
            row = table[pl.ds(pl.multiple_of(ids_s[0, r], 8), tiles), :]
            picked[pl.ds(pl.multiple_of(r * tiles, 8), tiles), :] = row
        return 0

    lax.fori_loop(0, rows // 8, pick, 0)

    source = lax.broadcasted_iota(jnp.int32, (COLS, LANES), 0) // width
    target = lax.broadcasted_iota(jnp.int32, (COLS, LANES), 1)
    spread = jnp.where((target % here == source) & (target < 3 * here), 1.0, 0.0).astype(
        jnp.bfloat16
    )

    def columns(j, _):
        at = pl.ds(pl.multiple_of(j * COLS, COLS), COLS)
        for i in range(rows // chunk):
            ra = slice(i * chunk, (i + 1) * chunk)
            near = jnp.concatenate(
                [
                    picked[pl.ds(i * chunk * tiles + j * side + h, chunk, stride=tiles), :]
                    for h in range(side)
                ],
                axis=1,
            )
            r = (arr_ref[ra, at].astype(jnp.float32) - near).astype(jnp.bfloat16)
            resid[ra, :] = r
            wide = r.astype(jnp.float32)
            square = wide * wide
            square_hi = square.astype(jnp.bfloat16)
            square_lo = (square - square_hi.astype(jnp.float32)).astype(jnp.bfloat16)
            n_hi, n_mid, n_lo = split3(dot(square_hi, spread) + dot(square_lo, spread))
            lane = lax.broadcasted_iota(jnp.int32, (chunk, LANES), 1)
            extra[ra, :] = jnp.where(
                lane < here,
                n_hi.astype(jnp.float32),
                jnp.where(
                    lane < 2 * here,
                    n_mid.astype(jnp.float32),
                    jnp.where(lane < 3 * here, n_lo.astype(jnp.float32), 1.0),
                ),
            ).astype(jnp.bfloat16)

        codes = code_t[j]
        level = lax.broadcasted_iota(jnp.int32, (levels, rows), 0)
        lane = lax.broadcasted_iota(jnp.int32, (levels, LANES), 1)
        extra_sum = jnp.zeros((levels, LANES), jnp.float32)
        pieces = []
        for part in range(side):
            weights = jnp.concatenate(
                [resid[:, part * LANES : (part + 1) * LANES], extra[...]], axis=1
            )
            sums = jnp.zeros((levels, LANES), jnp.float32)
            for k in range(group):
                i = part * group + k
                onehot = jnp.where(level == codes[i : i + 1], 1.0, 0.0).astype(jnp.bfloat16)
                found = dot(onehot, weights)
                sums = jnp.where(lane // width == k, found[:, :LANES], sums)
                extra_sum = jnp.where(lane % here == i, found[:, LANES:], extra_sum)
            pieces.append(jnp.transpose(sums))
        tail = jnp.transpose(extra_sum)
        norm_sum = (tail[:here] + tail[here : 2 * here]) + tail[2 * here : 3 * here]
        count_sum = tail[3 * here : 4 * here]
        steps = subs // parts // here
        for i in range(here):
            part, k = divmod(i, group)
            block = jnp.concatenate(
                [
                    pieces[part][k * width : (k + 1) * width],
                    count_sum[i : i + 1],
                    norm_sum[i : i + 1],
                ],
                axis=0,
            )
            left, right = block[:, :LANES], block[:, LANES:]
            at_row = ((lax.rem(j, steps) * here + i) * parts + lax.div(j, steps)) * held
            keep_ref[pl.ds(at_row, held), :] = jnp.where(first_core, left, right)
            give_ref[pl.ds(at_row, held), :] = jnp.where(first_core, right, left)
        return 0

    lax.fori_loop(0, dims // COLS, columns, 0)
    nc_copy.wait()


def local_pass(core, arrived, centroids, subs, width, prior, parts):
    rows = arrived.shape[0]
    lists, dims = centroids.shape
    tiles = dims // LANES
    here = COLS // width
    sums = jax.ShapeDtypeStruct((subs * (width + 2), LANES), jnp.float32)
    return pl.pallas_call(
        functools.partial(local_kernel, subs, width, parts, prior, 256),
        in_specs=[
            pl.BlockSpec(memory_space=pltpu.SMEM),
            IN_VMEM,
            IN_VMEM,
        ],
        out_specs=[pl.BlockSpec(memory_space=pl.ANY), IN_VMEM, IN_VMEM],
        out_shape=[jax.ShapeDtypeStruct((lists, dims), jnp.float32), sums, sums],
        scratch_shapes=[
            pltpu.VMEM((lists, rows), jnp.bfloat16),
            pltpu.VMEM((lists, LANES), jnp.float32),
            pltpu.VMEM((subs // here, here, rows), jnp.int32),
            pltpu.VMEM((lists * tiles, LANES), jnp.float32),
            pltpu.VMEM((rows * tiles, LANES), jnp.float32),
            pltpu.VMEM((rows, COLS), jnp.bfloat16),
            pltpu.VMEM((rows, LANES), jnp.bfloat16),
            pltpu.VMEM((1, rows), jnp.int32),
            pltpu.SMEM((1, rows), jnp.int32),
            pltpu.VMEM((lists, dims), jnp.float32),
            pltpu.SemaphoreType.DMA,
            pltpu.SemaphoreType.DMA,
        ],
        compiler_params=pltpu.CompilerParams(vmem_limit_bytes=32 * MIB),
        name="local_pass",
    )(core, arrived, centroids)


def owner_kernel(width, prior, copies, part_ref, old_ref, out_ref):
    held = width + 2
    sources = part_ref.shape[0] // held
    taken = [part_ref[pl.ds(i, sources, stride=held), :] for i in range(held)]
    sums, counts, norms = taken[:width], taken[width], taken[width + 1]
    count = jnp.sum(counts, axis=0, keepdims=True)
    share = 1.0 / jnp.maximum(counts, 1.0)
    inner = norms
    outer = jnp.zeros_like(norms)
    rows = []
    for d in range(width):
        total = jnp.sum(sums[d], axis=0, keepdims=True)
        new = (total + prior * old_ref[d : d + 1]) / (count + prior)
        mean = sums[d] * share
        gap = mean - new
        inner = inner - sums[d] * mean
        outer = outer + gap * gap
        rows.append(new)
    errors = jnp.sum(jnp.maximum(inner, 0.0) + counts * outer, axis=0, keepdims=True)
    rows.append(errors / (count + 1.0))
    result = jnp.concatenate(rows, axis=0)
    for c in range(copies):
        out_ref[c * (width + 1) : (c + 1) * (width + 1)] = result


def finish_kernel(width, core_ref, mine_ref, other_ref, table_ref, dist_ref):
    held = width + 1
    subs = table_ref.shape[0]
    first_core = core_ref[0] == 0
    for ref, at in ((0, slice(0, LANES)), (1, slice(LANES, 2 * LANES))):
        own = first_core if ref == 0 else jnp.logical_not(first_core)
        for m in range(subs):
            rows = slice(m * held, m * held + width)
            table_ref[m, :, at] = jnp.where(own, mine_ref[rows], other_ref[rows])
        last = pl.ds(width, subs, stride=held)
        dist_ref[:, at] = jnp.where(own, mine_ref[last, :], other_ref[last, :])


def on_device(vectors, list_ids, codes, centroids, codebooks):
    rows, dims = vectors.shape
    chips = lax.axis_size("chip")
    parts = lax.axis_size("sub")
    owners = chips * CORES * parts
    lists = centroids.shape[0]
    subs = codes.shape[1]
    my_subs, width, levels = codebooks.shape
    prior_lists = float(rows // lists)
    prior_codes = float(rows * owners // levels)
    core = lax.axis_index("core")
    core_arg = core.astype(jnp.int32).reshape(1)
    swap = [(0, 1), (1, 0)]

    sent, core_arg = lax.optimization_barrier((pack(vectors, list_ids, codes, lists), core_arg))
    arrived = lax.all_to_all(sent, SPLIT, split_axis=0, concat_axis=0, tiled=True)
    new_centroids, keep, give = local_pass(
        core_arg, arrived, centroids, subs, width, prior_lists, parts
    )
    paired = keep + lax.ppermute(give, "core", swap)
    held = width + 2
    mine = lax.all_to_all(
        paired.reshape(chips * parts, 1, held * LANES),
        ("chip", "sub"),
        split_axis=0,
        concat_axis=0,
        tiled=True,
    ).reshape(chips * parts * held, LANES)
    old = lax.dynamic_slice(
        codebooks, (lax.axis_index("chip"), 0, core * LANES), (1, width, LANES)
    )[0]
    held = width + 1
    done = pl.pallas_call(
        functools.partial(owner_kernel, width, prior_codes, chips),
        in_specs=[IN_VMEM, IN_VMEM],
        out_specs=IN_VMEM,
        out_shape=jax.ShapeDtypeStruct((chips * held, LANES), jnp.float32),
        compiler_params=pltpu.CompilerParams(vmem_limit_bytes=8 * MIB),
        name="owner_pass",
    )(mine, old)
    half = lax.all_to_all(
        done.reshape(chips, 1, held * LANES), "chip", split_axis=0, concat_axis=0, tiled=True
    ).reshape(chips * held, LANES)
    other = lax.ppermute(half, "core", swap)
    table, distortion = pl.pallas_call(
        functools.partial(finish_kernel, width),
        in_specs=[pl.BlockSpec(memory_space=pltpu.SMEM), IN_VMEM, IN_VMEM],
        out_specs=[IN_VMEM, IN_VMEM],
        out_shape=[
            jax.ShapeDtypeStruct((my_subs, width, levels), jnp.float32),
            jax.ShapeDtypeStruct((my_subs, levels), jnp.float32),
        ],
        compiler_params=pltpu.CompilerParams(vmem_limit_bytes=8 * MIB),
        name="finish",
    )(core_arg, half, other)
    return new_centroids, table, distortion


def solution(mesh):
    parts = mesh.shape["sub"]
    cores = Mesh(mesh.devices.reshape(-1, CORES, parts), SPLIT)
    in_specs = (
        P(SPLIT, None),
        P(SPLIT),
        P(SPLIT, None),
        P(SPLIT, None),
        P("sub", None, None),
    )
    out_specs = (P(SPLIT, None), P("sub", None, None), P("sub", None))
    return jax.shard_map(
        on_device, mesh=cores, in_specs=in_specs, out_specs=out_specs, check_vma=False
    )
```

```python
import functools

import jax
import jax.numpy as jnp
from jax import lax
from jax.experimental import pallas as pl
from jax.experimental.pallas import tpu as pltpu
from jax.sharding import Mesh, PartitionSpec as P

LANES = 128
COLS = 256
CORES = 2
MIB = 1024 * 1024
IN_VMEM = pl.BlockSpec(memory_space=pltpu.VMEM)
SPLIT = ("chip", "core", "sub")


def split3(x):
    hi = x.astype(jnp.bfloat16)
    rest = x - hi.astype(jnp.float32)
    mid = rest.astype(jnp.bfloat16)
    lo = (rest - mid.astype(jnp.float32)).astype(jnp.bfloat16)
    return hi, mid, lo


def dot(a, b):
    return jnp.dot(a, b, preferred_element_type=jnp.float32)


def pack_kernel(
    lists, pieces, v_ref, ids_ref, codes_ref, out_ref, held, ids_v, codes_v, ins, outs
):
    rows, dims = v_ref.shape
    subs = codes_ref.shape[0]
    step = rows // pieces
    first = [
        pltpu.make_async_copy(codes_ref, codes_v, ins.at[pieces]),
        pltpu.make_async_copy(ids_ref, ids_v, ins.at[pieces + 1]),
    ]
    moves = [
        pltpu.make_async_copy(
            v_ref.at[pl.ds(i * step, step)],
            held.at[pl.ds(i * step, step), pl.ds(0, dims)],
            ins.at[i],
        )
        for i in range(pieces)
    ]
    for move in first + moves:
        move.start()
    for move in first:
        move.wait()
    ids = lax.rem(ids_v[...], lists)
    high = lax.div(ids, 256)
    aux = jnp.concatenate(
        [
            codes_v[...].astype(jnp.float32),
            high.astype(jnp.float32),
            (ids - 256 * high).astype(jnp.float32),
            jnp.zeros((LANES - subs - 2, rows), jnp.float32),
        ],
        axis=0,
    )
    held[:, dims:] = jnp.transpose(aux).astype(jnp.bfloat16)
    sends = []
    for i, move in enumerate(moves):
        move.wait()
        at = pl.ds(i * step, step)
        send = pltpu.make_async_copy(held.at[at], out_ref.at[at], outs.at[i])
        send.start()
        sends.append(send)
    for send in sends:
        send.wait()


def pack(vectors, list_ids, codes, lists):
    rows, dims = vectors.shape
    subs = codes.shape[1]
    pieces = 8
    anywhere = pl.BlockSpec(memory_space=pl.ANY)
    return pl.pallas_call(
        functools.partial(pack_kernel, lists, pieces),
        in_specs=[anywhere] * 3,
        out_specs=anywhere,
        out_shape=jax.ShapeDtypeStruct((rows, dims + LANES), jnp.bfloat16),
        scratch_shapes=[
            pltpu.VMEM((rows, dims + LANES), jnp.bfloat16),
            pltpu.VMEM((1, rows), jnp.int32),
            pltpu.VMEM((subs, rows), jnp.int32),
            pltpu.SemaphoreType.DMA((pieces + 2,)),
            pltpu.SemaphoreType.DMA((pieces,)),
        ],
        compiler_params=pltpu.CompilerParams(vmem_limit_bytes=58 * MIB),
        name="pack",
    )(vectors, list_ids.reshape(1, rows), jnp.transpose(codes))


def local_kernel(
    subs,
    width,
    parts,
    prior,
    chunk,
    core_ref,
    arr_ref,
    cent_ref,
    nc_ref,
    keep_ref,
    give_ref,
    hot,
    inv,
    code_t,
    table,
    picked,
    low_v,
    high_v,
    norms,
    side_v,
    extra,
    ids_v,
    ids_s,
    nc_v,
    sem,
    nc_sem,
):
    rows = arr_ref.shape[0]
    lists, dims = cent_ref.shape
    tiles = dims // LANES
    here = COLS // width
    group = LANES // width
    side = COLS // LANES
    held = width + 2
    quad = group // 2
    kinds = 4
    first_core = core_ref[0] == 0

    aux = arr_ref[:, dims:]
    aux_t = jnp.transpose(aux.astype(jnp.float32))
    row_ids = (aux_t[subs : subs + 1] * 256.0 + aux_t[subs + 1 : subs + 2]).astype(jnp.int32)
    ids_v[...] = row_ids * tiles
    copy = pltpu.make_async_copy(ids_v, ids_s, sem)
    copy.start()
    level = lax.broadcasted_iota(jnp.int32, (lists, rows), 0)
    hot[...] = jnp.where(level == row_ids, 1.0, 0.0).astype(jnp.bfloat16)
    counts = dot(hot[...], jnp.ones((rows, LANES), jnp.bfloat16))
    inv[...] = 1.0 / (counts + prior)
    for b in range(subs // group):
        block = aux_t[b * group : (b + 1) * group].astype(jnp.int32)
        code_t[b] = jnp.where(block < LANES, block, block - LANES)
    line = lax.broadcasted_iota(jnp.int32, (LANES, LANES), 0)
    lane = lax.broadcasted_iota(jnp.int32, (LANES, LANES), 1)
    twice = jnp.where(line == lax.rem(lane, subs), 1.0, 0.0).astype(jnp.bfloat16)
    both = dot(aux, twice)
    lane = lax.broadcasted_iota(jnp.int32, (rows, LANES), 1)
    inside = jnp.where((both < LANES) == (lane < subs), 1.0, 0.0)
    side_v[:, 3 * LANES :] = inside.astype(jnp.bfloat16)

    for j in range(dims // COLS):
        totals = dot(hot[...], arr_ref[:, j * COLS : (j + 1) * COLS])
        for h in range(side):
            tile = j * side + h
            at = slice(tile * LANES, (tile + 1) * LANES)
            old = prior * cent_ref[:, at].astype(jnp.float32)
            nc = (totals[:, h * LANES : (h + 1) * LANES] + old) * inv[...]
            nc_v[:, at] = nc
            table[pl.ds(tile, lists, stride=tiles), :] = nc
    nc_copy = pltpu.make_async_copy(nc_v, nc_ref, nc_sem)
    nc_copy.start()
    copy.wait()

    def pick(q, _):
        for u in range(8):
            r = q * 8 + u
            row = table[pl.ds(pl.multiple_of(ids_s[0, r], 8), tiles), :]
            picked[pl.ds(pl.multiple_of(r * tiles, 8), tiles), :] = row
        return 0

    lax.fori_loop(0, rows // 8, pick, 0)

    def residuals(j, _):
        at = pl.ds(pl.multiple_of(j * COLS, COLS), COLS)
        line = lax.broadcasted_iota(jnp.int32, (LANES, COLS), 0)
        column = lax.broadcasted_iota(jnp.int32, (LANES, COLS), 1)
        widen = jnp.where(line == j * here + column // width, 1.0, 0.0).astype(jnp.bfloat16)
        line = lax.broadcasted_iota(jnp.int32, (COLS, LANES), 0)
        column = lax.broadcasted_iota(jnp.int32, (COLS, LANES), 1)
        fold = jnp.where(
            lax.rem(column, subs) == j * here + line // width, 1.0, 0.0
        ).astype(jnp.bfloat16)
        for i in range(rows // chunk):
            ra = slice(i * chunk, (i + 1) * chunk)
            near = jnp.concatenate(
                [
                    picked[pl.ds(i * chunk * tiles + j * side + h, chunk, stride=tiles), :]
                    for h in range(side)
                ],
                axis=1,
            )
            r = (arr_ref[ra, at].astype(jnp.float32) - near).astype(jnp.bfloat16)
            wide = r.astype(jnp.float32)
            low = r * dot(side_v[ra, 3 * LANES :], widen).astype(jnp.bfloat16)
            low_v[ra, at] = low
            high_v[ra, at] = r - low
            square = wide * wide
            square_hi = square.astype(jnp.bfloat16)
            square_lo = (square - square_hi.astype(jnp.float32)).astype(jnp.bfloat16)
            found = dot(square_hi, fold) + dot(square_lo, fold)
            norms[ra, :] = jnp.where(j == 0, found, norms[ra, :] + found)
        return 0

    lax.fori_loop(0, dims // COLS, residuals, 0)

    for i in range(rows // chunk):
        ra = slice(i * chunk, (i + 1) * chunk)
        pieces = split3(norms[ra, :] * side_v[ra, 3 * LANES :].astype(jnp.float32))
        for k, piece in enumerate(pieces):
            side_v[ra, k * LANES : (k + 1) * LANES] = piece

    def columns(j, _):
        line = lax.broadcasted_iota(jnp.int32, (kinds * LANES, COLS), 0)
        column = lax.broadcasted_iota(jnp.int32, (kinds * LANES, COLS), 1)
        spot = lax.rem(column, LANES // 2)
        in_first = lax.rem(column, LANES) >= LANES // 2
        kind = spot // (2 * quad)
        half = lax.rem(spot, 2 * quad) // quad
        sub = (
            j * here
            + (column // LANES) * group
            + jnp.where(in_first, 0, quad)
            + lax.rem(spot, quad)
        )
        wanted = kind * LANES + half * subs + sub
        move = jnp.where((line == wanted) & (kind < kinds), 1.0, 0.0).astype(jnp.bfloat16)
        for i in range(rows // chunk):
            ra = slice(i * chunk, (i + 1) * chunk)
            extra[ra, :] = dot(side_v[ra, :], move).astype(jnp.bfloat16)

        level = lax.broadcasted_iota(jnp.int32, (LANES, rows), 0)
        lane = lax.broadcasted_iota(jnp.int32, (LANES, LANES), 1)
        wide_lane = lax.broadcasted_iota(jnp.int32, (rows, LANES), 1)
        steps = subs // parts // here
        for part in range(side):
            at = pl.ds(pl.multiple_of(j * COLS + part * LANES, LANES), LANES)
            codes = code_t[j * side + part]
            codes16 = codes.astype(jnp.float32).astype(jnp.bfloat16)
            level16 = level.astype(jnp.float32).astype(jnp.bfloat16)
            beside = extra[:, part * LANES : (part + 1) * LANES]
            low_sum = jnp.zeros((LANES, LANES), jnp.float32)
            high_sum = low_sum
            extra_sum = low_sum
            for q in range(2):
                own = (wide_lane < LANES // 2) == (q == 0)
                mixed = jnp.where(own, high_v[:, at], beside)
                weights = jnp.concatenate([low_v[:, at], mixed], axis=1)
                apart = (lane >= LANES // 2) == (q == 0)
                onehot = jnp.concatenate(
                    [
                        jnp.where(level16 == codes16[i : i + 1], jnp.ones((), jnp.bfloat16), jnp.zeros((), jnp.bfloat16))
                        for i in range(q * quad, (q + 1) * quad)
                    ],
                    axis=0,
                )
                every = dot(onehot, weights)
                for k in range(quad):
                    i = q * quad + k
                    found = every[k * LANES : (k + 1) * LANES]
                    low_sum = jnp.where(lane // width == i, found[:, :LANES], low_sum)
                    high_sum = jnp.where(lane // width == i, found[:, LANES:], high_sum)
                    extra_sum = jnp.where(
                        apart & (lax.rem(lane, quad) == k), found[:, LANES:], extra_sum
                    )
            low_t = jnp.transpose(low_sum)
            high_t = jnp.transpose(high_sum)
            extra_t = jnp.transpose(extra_sum)
            for i in range(group):
                q, k = divmod(i, quad)
                base = LANES // 2 if q == 0 else 0
                blocks = []
                for half, sums in ((0, low_t), (1, high_t)):
                    found = [
                        extra_t[row : row + 1]
                        for row in range(base + half * quad + k, base + LANES // 2, 2 * quad)
                    ]
                    norm = (found[0] + found[1]) + found[2]
                    blocks.append(
                        jnp.concatenate(
                            [sums[i * width : (i + 1) * width], found[3], norm], axis=0
                        )
                    )
                sub = lax.rem(j, steps) * here + part * group + i
                at_row = (sub * parts + lax.div(j, steps)) * held
                keep_ref[pl.ds(at_row, held), :] = jnp.where(first_core, blocks[0], blocks[1])
                give_ref[pl.ds(at_row, held), :] = jnp.where(first_core, blocks[1], blocks[0])
        return 0

    for j in range(dims // COLS):
        columns(j, 0)
    nc_copy.wait()


def local_pass(core, arrived, centroids, subs, width, prior, parts):
    rows = arrived.shape[0]
    lists, dims = centroids.shape
    tiles = dims // LANES
    group = LANES // width
    sums = jax.ShapeDtypeStruct((subs * (width + 2), LANES), jnp.float32)
    return pl.pallas_call(
        functools.partial(local_kernel, subs, width, parts, prior, 256),
        in_specs=[pl.BlockSpec(memory_space=pltpu.SMEM), IN_VMEM, IN_VMEM],
        out_specs=[pl.BlockSpec(memory_space=pl.ANY), IN_VMEM, IN_VMEM],
        out_shape=[jax.ShapeDtypeStruct((lists, dims), jnp.float32), sums, sums],
        scratch_shapes=[
            pltpu.VMEM((lists, rows), jnp.bfloat16),
            pltpu.VMEM((lists, LANES), jnp.float32),
            pltpu.VMEM((subs // group, group, rows), jnp.int32),
            pltpu.VMEM((lists * tiles, LANES), jnp.float32),
            pltpu.VMEM((rows * tiles, LANES), jnp.float32),
            pltpu.VMEM((rows, dims), jnp.bfloat16),
            pltpu.VMEM((rows, dims), jnp.bfloat16),
            pltpu.VMEM((rows, LANES), jnp.float32),
            pltpu.VMEM((rows, 4 * LANES), jnp.bfloat16),
            pltpu.VMEM((rows, COLS), jnp.bfloat16),
            pltpu.VMEM((1, rows), jnp.int32),
            pltpu.SMEM((1, rows), jnp.int32),
            pltpu.VMEM((lists, dims), jnp.float32),
            pltpu.SemaphoreType.DMA,
            pltpu.SemaphoreType.DMA,
        ],
        compiler_params=pltpu.CompilerParams(vmem_limit_bytes=32 * MIB),
        name="local_pass",
    )(core, arrived, centroids)


def owner_kernel(width, prior, copies, part_ref, old_ref, out_ref):
    held = width + 2
    sources = part_ref.shape[0] // held
    taken = [part_ref[pl.ds(i, sources, stride=held), :] for i in range(held)]
    sums, counts, norms = taken[:width], taken[width], taken[width + 1]
    count = jnp.sum(counts, axis=0, keepdims=True)
    share = 1.0 / jnp.maximum(counts, 1.0)
    inner = norms
    outer = jnp.zeros_like(norms)
    rows = []
    for d in range(width):
        total = jnp.sum(sums[d], axis=0, keepdims=True)
        new = (total + prior * old_ref[d : d + 1]) / (count + prior)
        mean = sums[d] * share
        gap = mean - new
        inner = inner - sums[d] * mean
        outer = outer + gap * gap
        rows.append(new)
    errors = jnp.sum(jnp.maximum(inner, 0.0) + counts * outer, axis=0, keepdims=True)
    rows.append(errors / (count + 1.0))
    result = jnp.concatenate(rows, axis=0)
    for c in range(copies):
        out_ref[c * (width + 1) : (c + 1) * (width + 1)] = result


def finish_kernel(width, core_ref, mine_ref, other_ref, table_ref, dist_ref):
    held = width + 1
    subs = table_ref.shape[0]
    first_core = core_ref[0] == 0
    for ref, at in ((0, slice(0, LANES)), (1, slice(LANES, 2 * LANES))):
        own = first_core if ref == 0 else jnp.logical_not(first_core)
        for m in range(subs):
            rows = slice(m * held, m * held + width)
            table_ref[m, :, at] = jnp.where(own, mine_ref[rows], other_ref[rows])
        last = pl.ds(width, subs, stride=held)
        dist_ref[:, at] = jnp.where(own, mine_ref[last, :], other_ref[last, :])


def on_device(vectors, list_ids, codes, centroids, codebooks):
    rows, dims = vectors.shape
    chips = lax.axis_size("chip")
    parts = lax.axis_size("sub")
    owners = chips * CORES * parts
    lists = centroids.shape[0]
    subs = codes.shape[1]
    my_subs, width, levels = codebooks.shape
    prior_lists = float(rows // lists)
    prior_codes = float(rows * owners // levels)
    core = lax.axis_index("core")
    core_arg = core.astype(jnp.int32).reshape(1)
    swap = [(0, 1), (1, 0)]

    sent, core_arg = lax.optimization_barrier((pack(vectors, list_ids, codes, lists), core_arg))
    arrived = lax.all_to_all(sent, SPLIT, split_axis=0, concat_axis=0, tiled=True)
    new_centroids, keep, give = local_pass(
        core_arg, arrived, centroids, subs, width, prior_lists, parts
    )
    paired = keep + lax.ppermute(give, "core", swap)
    held = width + 2
    mine = lax.all_to_all(
        paired.reshape(chips * parts, 1, held * LANES),
        ("chip", "sub"),
        split_axis=0,
        concat_axis=0,
        tiled=True,
    ).reshape(chips * parts * held, LANES)
    old = lax.dynamic_slice(
        codebooks, (lax.axis_index("chip"), 0, core * LANES), (1, width, LANES)
    )[0]
    held = width + 1
    done = pl.pallas_call(
        functools.partial(owner_kernel, width, prior_codes, chips),
        in_specs=[IN_VMEM, IN_VMEM],
        out_specs=IN_VMEM,
        out_shape=jax.ShapeDtypeStruct((chips * held, LANES), jnp.float32),
        compiler_params=pltpu.CompilerParams(vmem_limit_bytes=8 * MIB),
        name="owner_pass",
    )(mine, old)
    half = lax.all_to_all(
        done.reshape(chips, 1, held * LANES), "chip", split_axis=0, concat_axis=0, tiled=True
    ).reshape(chips * held, LANES)
    other = lax.ppermute(half, "core", swap)
    table, distortion = pl.pallas_call(
        functools.partial(finish_kernel, width),
        in_specs=[pl.BlockSpec(memory_space=pltpu.SMEM), IN_VMEM, IN_VMEM],
        out_specs=[IN_VMEM, IN_VMEM],
        out_shape=[
            jax.ShapeDtypeStruct((my_subs, width, levels), jnp.float32),
            jax.ShapeDtypeStruct((my_subs, levels), jnp.float32),
        ],
        compiler_params=pltpu.CompilerParams(vmem_limit_bytes=8 * MIB),
        name="finish",
    )(core_arg, half, other)
    return new_centroids, table, distortion


def solution(mesh):
    parts = mesh.shape["sub"]
    cores = Mesh(mesh.devices.reshape(-1, CORES, parts), SPLIT)
    in_specs = (
        P(SPLIT, None),
        P(SPLIT),
        P(SPLIT, None),
        P(SPLIT, None),
        P("sub", None, None),
    )
    out_specs = (P(SPLIT, None), P("sub", None, None), P("sub", None))
    return jax.shard_map(
        on_device, mesh=cores, in_specs=in_specs, out_specs=out_specs, check_vma=False
    )
```

```python
import functools

import jax
import jax.numpy as jnp
from jax import lax
from jax.experimental import pallas as pl
from jax.experimental.pallas import tpu as pltpu
from jax.sharding import Mesh, PartitionSpec as P

LANES = 128
COLS = 256
CORES = 2
MIB = 1024 * 1024
IN_VMEM = pl.BlockSpec(memory_space=pltpu.VMEM)
SPLIT = ("chip", "core", "sub")


def split3(x):
    hi = x.astype(jnp.bfloat16)
    rest = x - hi.astype(jnp.float32)
    mid = rest.astype(jnp.bfloat16)
    lo = (rest - mid.astype(jnp.float32)).astype(jnp.bfloat16)
    return hi, mid, lo


def dot(a, b):
    return jnp.dot(a, b, preferred_element_type=jnp.float32)


def pack_kernel(
    lists, pieces, place, v_ref, ids_ref, codes_ref, books_ref, out_ref, old_ref, ids_v, codes_v, sems
):
    rows, dims = v_ref.shape
    subs = codes_ref.shape[0]
    step = rows // pieces
    half = pl.ds(pl.multiple_of(place[1] * LANES, LANES), LANES)
    small = [
        pltpu.make_async_copy(codes_ref, codes_v, sems.at[pieces]),
        pltpu.make_async_copy(ids_ref, ids_v, sems.at[pieces + 1]),
    ]
    moves = [
        pltpu.make_async_copy(
            v_ref.at[pl.ds(i * step, step)],
            out_ref.at[pl.ds(i * step, step), pl.ds(0, dims)],
            sems.at[i],
        )
        for i in range(pieces)
    ]
    moves.append(
        pltpu.make_async_copy(books_ref.at[place[0], :, half], old_ref, sems.at[pieces + 2])
    )
    for move in small + moves:
        move.start()
    for move in small:
        move.wait()
    ids = lax.rem(ids_v[...], lists)
    high = lax.div(ids, 256)
    aux = jnp.concatenate(
        [
            codes_v[...].astype(jnp.float32),
            high.astype(jnp.float32),
            (ids - 256 * high).astype(jnp.float32),
            jnp.zeros((LANES - subs - 2, rows), jnp.float32),
        ],
        axis=0,
    )
    out_ref[:, dims:] = jnp.transpose(aux).astype(jnp.bfloat16)
    for move in moves:
        move.wait()


def pack(place, vectors, list_ids, codes, codebooks, lists):
    rows, dims = vectors.shape
    subs = codes.shape[1]
    width = codebooks.shape[1]
    pieces = 4
    anywhere = pl.BlockSpec(memory_space=pl.ANY)
    sources = (vectors, list_ids.reshape(1, rows), jnp.transpose(codes), codebooks)
    return pl.pallas_call(
        functools.partial(pack_kernel, lists, pieces),
        in_specs=[pl.BlockSpec(memory_space=pltpu.SMEM)] + [anywhere] * 4,
        out_specs=[IN_VMEM, IN_VMEM],
        out_shape=[
            jax.ShapeDtypeStruct((rows, dims + LANES), jnp.bfloat16),
            jax.ShapeDtypeStruct((width, LANES), jnp.float32),
        ],
        scratch_shapes=[
            pltpu.VMEM((1, rows), jnp.int32),
            pltpu.VMEM((subs, rows), jnp.int32),
            pltpu.SemaphoreType.DMA((pieces + 3,)),
        ],
        compiler_params=pltpu.CompilerParams(vmem_limit_bytes=12 * MIB),
        name="pack",
    )(place, *[pltpu.with_memory_space_constraint(x, pltpu.HBM) for x in sources])


def local_kernel(
    subs,
    width,
    parts,
    prior,
    chunk,
    core_ref,
    arr_ref,
    cent_ref,
    nc_ref,
    keep_ref,
    give_ref,
    hot,
    inv,
    code_t,
    table,
    picked,
    low_v,
    high_v,
    norms,
    side_v,
    extra,
    ids_v,
    ids_s,
    nc_v,
    sem,
    nc_sem,
):
    rows = arr_ref.shape[0]
    lists, dims = cent_ref.shape
    tiles = dims // LANES
    here = COLS // width
    group = LANES // width
    side = COLS // LANES
    held = width + 2
    quad = group // 2
    kinds = 4
    first_core = core_ref[0] == 0

    aux = arr_ref[:, dims:]
    aux_t = jnp.transpose(aux.astype(jnp.float32))
    row_ids = (aux_t[subs : subs + 1] * 256.0 + aux_t[subs + 1 : subs + 2]).astype(jnp.int32)
    ids_v[...] = row_ids * tiles
    copy = pltpu.make_async_copy(ids_v, ids_s, sem)
    copy.start()
    level = lax.broadcasted_iota(jnp.int32, (lists, rows), 0)
    hot[...] = jnp.where(level == row_ids, 1.0, 0.0).astype(jnp.bfloat16)
    counts = dot(hot[...], jnp.ones((rows, LANES), jnp.bfloat16))
    inv[...] = 1.0 / (counts + prior)
    for b in range(subs // group):
        block = aux_t[b * group : (b + 1) * group].astype(jnp.int32)
        code_t[b] = jnp.where(block < LANES, block, block - LANES)
    line = lax.broadcasted_iota(jnp.int32, (LANES, LANES), 0)
    lane = lax.broadcasted_iota(jnp.int32, (LANES, LANES), 1)
    twice = jnp.where(line == lax.rem(lane, subs), 1.0, 0.0).astype(jnp.bfloat16)
    both = dot(aux, twice)
    lane = lax.broadcasted_iota(jnp.int32, (rows, LANES), 1)
    inside = jnp.where((both < LANES) == (lane < subs), 1.0, 0.0)
    side_v[:, 3 * LANES :] = inside.astype(jnp.bfloat16)

    for j in range(dims // COLS):
        totals = dot(hot[...], arr_ref[:, j * COLS : (j + 1) * COLS])
        for h in range(side):
            tile = j * side + h
            at = slice(tile * LANES, (tile + 1) * LANES)
            old = prior * cent_ref[:, at].astype(jnp.float32)
            nc = (totals[:, h * LANES : (h + 1) * LANES] + old) * inv[...]
            nc_v[:, at] = nc
            table[pl.ds(tile, lists, stride=tiles), :] = nc
    nc_copy = pltpu.make_async_copy(nc_v, nc_ref, nc_sem)
    nc_copy.start()
    copy.wait()

    def pick(q, _):
        for u in range(8):
            r = q * 8 + u
            row = table[pl.ds(pl.multiple_of(ids_s[0, r], 8), tiles), :]
            picked[pl.ds(pl.multiple_of(r * tiles, 8), tiles), :] = row
        return 0

    lax.fori_loop(0, rows // 8, pick, 0)

    def residuals(j, _):
        at = pl.ds(pl.multiple_of(j * COLS, COLS), COLS)
        line = lax.broadcasted_iota(jnp.int32, (LANES, COLS), 0)
        column = lax.broadcasted_iota(jnp.int32, (LANES, COLS), 1)
        widen = jnp.where(line == j * here + column // width, 1.0, 0.0).astype(jnp.bfloat16)
        line = lax.broadcasted_iota(jnp.int32, (COLS, LANES), 0)
        column = lax.broadcasted_iota(jnp.int32, (COLS, LANES), 1)
        fold = jnp.where(
            lax.rem(column, subs) == j * here + line // width, 1.0, 0.0
        ).astype(jnp.bfloat16)
        for i in range(rows // chunk):
            ra = slice(i * chunk, (i + 1) * chunk)
            near = jnp.concatenate(
                [
                    picked[pl.ds(i * chunk * tiles + j * side + h, chunk, stride=tiles), :]
                    for h in range(side)
                ],
                axis=1,
            )
            r = (arr_ref[ra, at].astype(jnp.float32) - near).astype(jnp.bfloat16)
            wide = r.astype(jnp.float32)
            low = r * dot(side_v[ra, 3 * LANES :], widen).astype(jnp.bfloat16)
            low_v[ra, at] = low
            high_v[ra, at] = r - low
            square = wide * wide
            square_hi = square.astype(jnp.bfloat16)
            square_lo = (square - square_hi.astype(jnp.float32)).astype(jnp.bfloat16)
            found = dot(square_hi, fold) + dot(square_lo, fold)
            norms[ra, :] = jnp.where(j == 0, found, norms[ra, :] + found)
        return 0

    lax.fori_loop(0, dims // COLS, residuals, 0)

    for i in range(rows // chunk):
        ra = slice(i * chunk, (i + 1) * chunk)
        pieces = split3(norms[ra, :] * side_v[ra, 3 * LANES :].astype(jnp.float32))
        for k, piece in enumerate(pieces):
            side_v[ra, k * LANES : (k + 1) * LANES] = piece

    def columns(j, _):
        line = lax.broadcasted_iota(jnp.int32, (kinds * LANES, COLS), 0)
        column = lax.broadcasted_iota(jnp.int32, (kinds * LANES, COLS), 1)
        spot = lax.rem(column, LANES // 2)
        in_first = lax.rem(column, LANES) >= LANES // 2
        kind = spot // (2 * quad)
        half = lax.rem(spot, 2 * quad) // quad
        sub = (
            j * here
            + (column // LANES) * group
            + jnp.where(in_first, 0, quad)
            + lax.rem(spot, quad)
        )
        wanted = kind * LANES + half * subs + sub
        move = jnp.where((line == wanted) & (kind < kinds), 1.0, 0.0).astype(jnp.bfloat16)
        for i in range(rows // chunk):
            ra = slice(i * chunk, (i + 1) * chunk)
            extra[ra, :] = dot(side_v[ra, :], move).astype(jnp.bfloat16)

        level = lax.broadcasted_iota(jnp.int32, (LANES, rows), 0)
        lane = lax.broadcasted_iota(jnp.int32, (LANES, LANES), 1)
        wide_lane = lax.broadcasted_iota(jnp.int32, (rows, LANES), 1)
        steps = subs // parts // here
        for part in range(side):
            at = pl.ds(pl.multiple_of(j * COLS + part * LANES, LANES), LANES)
            codes = code_t[j * side + part]
            codes16 = codes.astype(jnp.float32).astype(jnp.bfloat16)
            level16 = level.astype(jnp.float32).astype(jnp.bfloat16)
            beside = extra[:, part * LANES : (part + 1) * LANES]
            low_sum = jnp.zeros((LANES, LANES), jnp.float32)
            high_sum = low_sum
            extra_sum = low_sum
            for q in range(2):
                own = (wide_lane < LANES // 2) == (q == 0)
                mixed = jnp.where(own, high_v[:, at], beside)
                weights = jnp.concatenate([low_v[:, at], mixed], axis=1)
                apart = (lane >= LANES // 2) == (q == 0)
                onehot = jnp.concatenate(
                    [
                        jnp.where(level16 == codes16[i : i + 1], jnp.ones((), jnp.bfloat16), jnp.zeros((), jnp.bfloat16))
                        for i in range(q * quad, (q + 1) * quad)
                    ],
                    axis=0,
                )
                every = dot(onehot, weights)
                for k in range(quad):
                    i = q * quad + k
                    found = every[k * LANES : (k + 1) * LANES]
                    low_sum = jnp.where(lane // width == i, found[:, :LANES], low_sum)
                    high_sum = jnp.where(lane // width == i, found[:, LANES:], high_sum)
                    extra_sum = jnp.where(
                        apart & (lax.rem(lane, quad) == k), found[:, LANES:], extra_sum
                    )
            low_t = jnp.transpose(low_sum)
            high_t = jnp.transpose(high_sum)
            extra_t = jnp.transpose(extra_sum)
            for i in range(group):
                q, k = divmod(i, quad)
                base = LANES // 2 if q == 0 else 0
                blocks = []
                for half, sums in ((0, low_t), (1, high_t)):
                    found = [
                        extra_t[row : row + 1]
                        for row in range(base + half * quad + k, base + LANES // 2, 2 * quad)
                    ]
                    norm = (found[0] + found[1]) + found[2]
                    blocks.append(
                        jnp.concatenate(
                            [sums[i * width : (i + 1) * width], found[3], norm], axis=0
                        )
                    )
                sub = lax.rem(j, steps) * here + part * group + i
                at_row = (sub * parts + lax.div(j, steps)) * held
                keep_ref[pl.ds(at_row, held), :] = jnp.where(first_core, blocks[0], blocks[1])
                give_ref[pl.ds(at_row, held), :] = jnp.where(first_core, blocks[1], blocks[0])
        return 0

    for j in range(dims // COLS):
        columns(j, 0)
    nc_copy.wait()


def local_pass(core, arrived, centroids, subs, width, prior, parts):
    rows = arrived.shape[0]
    lists, dims = centroids.shape
    tiles = dims // LANES
    group = LANES // width
    sums = jax.ShapeDtypeStruct((subs * (width + 2), LANES), jnp.float32)
    return pl.pallas_call(
        functools.partial(local_kernel, subs, width, parts, prior, 256),
        in_specs=[pl.BlockSpec(memory_space=pltpu.SMEM), IN_VMEM, IN_VMEM],
        out_specs=[pl.BlockSpec(memory_space=pl.ANY), IN_VMEM, IN_VMEM],
        out_shape=[jax.ShapeDtypeStruct((lists, dims), jnp.float32), sums, sums],
        scratch_shapes=[
            pltpu.VMEM((lists, rows), jnp.bfloat16),
            pltpu.VMEM((lists, LANES), jnp.float32),
            pltpu.VMEM((subs // group, group, rows), jnp.int32),
            pltpu.VMEM((lists * tiles, LANES), jnp.float32),
            pltpu.VMEM((rows * tiles, LANES), jnp.float32),
            pltpu.VMEM((rows, dims), jnp.bfloat16),
            pltpu.VMEM((rows, dims), jnp.bfloat16),
            pltpu.VMEM((rows, LANES), jnp.float32),
            pltpu.VMEM((rows, 4 * LANES), jnp.bfloat16),
            pltpu.VMEM((rows, COLS), jnp.bfloat16),
            pltpu.VMEM((1, rows), jnp.int32),
            pltpu.SMEM((1, rows), jnp.int32),
            pltpu.VMEM((lists, dims), jnp.float32),
            pltpu.SemaphoreType.DMA,
            pltpu.SemaphoreType.DMA,
        ],
        compiler_params=pltpu.CompilerParams(vmem_limit_bytes=32 * MIB),
        name="local_pass",
    )(core, arrived, centroids)


def owner_kernel(width, prior, copies, part_ref, old_ref, out_ref):
    held = width + 2
    sources = part_ref.shape[0] // held
    taken = [part_ref[pl.ds(i, sources, stride=held), :] for i in range(held)]
    sums, counts, norms = taken[:width], taken[width], taken[width + 1]
    count = jnp.sum(counts, axis=0, keepdims=True)
    share = 1.0 / jnp.maximum(counts, 1.0)
    inner = norms
    outer = jnp.zeros_like(norms)
    rows = []
    for d in range(width):
        total = jnp.sum(sums[d], axis=0, keepdims=True)
        new = (total + prior * old_ref[d : d + 1]) / (count + prior)
        mean = sums[d] * share
        gap = mean - new
        inner = inner - sums[d] * mean
        outer = outer + gap * gap
        rows.append(new)
    errors = jnp.sum(jnp.maximum(inner, 0.0) + counts * outer, axis=0, keepdims=True)
    rows.append(errors / (count + 1.0))
    result = jnp.concatenate(rows, axis=0)
    for c in range(copies):
        out_ref[c * (width + 1) : (c + 1) * (width + 1)] = result


def finish_kernel(width, core_ref, mine_ref, other_ref, table_ref, dist_ref):
    held = width + 1
    subs = table_ref.shape[0]
    first_core = core_ref[0] == 0
    for ref, at in ((0, slice(0, LANES)), (1, slice(LANES, 2 * LANES))):
        own = first_core if ref == 0 else jnp.logical_not(first_core)
        for m in range(subs):
            rows = slice(m * held, m * held + width)
            table_ref[m, :, at] = jnp.where(own, mine_ref[rows], other_ref[rows])
        last = pl.ds(width, subs, stride=held)
        dist_ref[:, at] = jnp.where(own, mine_ref[last, :], other_ref[last, :])


def on_device(vectors, list_ids, codes, centroids, codebooks):
    rows, dims = vectors.shape
    chips = lax.axis_size("chip")
    parts = lax.axis_size("sub")
    owners = chips * CORES * parts
    lists = centroids.shape[0]
    subs = codes.shape[1]
    my_subs, width, levels = codebooks.shape
    prior_lists = float(rows // lists)
    prior_codes = float(rows * owners // levels)
    core = lax.axis_index("core")
    core_arg = core.astype(jnp.int32).reshape(1)
    swap = [(0, 1), (1, 0)]

    place = jnp.stack([lax.axis_index("chip"), core]).astype(jnp.int32)
    sent, old = pack(place, vectors, list_ids, codes, codebooks, lists)
    arrived = lax.all_to_all(sent, SPLIT, split_axis=0, concat_axis=0, tiled=True)
    new_centroids, keep, give = local_pass(
        core_arg, arrived, centroids, subs, width, prior_lists, parts
    )
    paired = keep + lax.ppermute(give, "core", swap)
    held = width + 2
    mine = lax.all_to_all(
        paired.reshape(chips * parts, 1, held * LANES),
        ("chip", "sub"),
        split_axis=0,
        concat_axis=0,
        tiled=True,
    ).reshape(chips * parts * held, LANES)
    held = width + 1
    done = pl.pallas_call(
        functools.partial(owner_kernel, width, prior_codes, chips),
        in_specs=[IN_VMEM, IN_VMEM],
        out_specs=IN_VMEM,
        out_shape=jax.ShapeDtypeStruct((chips * held, LANES), jnp.float32),
        compiler_params=pltpu.CompilerParams(vmem_limit_bytes=8 * MIB),
        name="owner_pass",
    )(mine, old)
    half = lax.all_to_all(
        done.reshape(chips, 1, held * LANES), "chip", split_axis=0, concat_axis=0, tiled=True
    ).reshape(chips * held, LANES)
    other = lax.ppermute(half, "core", swap)
    table, distortion = pl.pallas_call(
        functools.partial(finish_kernel, width),
        in_specs=[pl.BlockSpec(memory_space=pltpu.SMEM), IN_VMEM, IN_VMEM],
        out_specs=[IN_VMEM, IN_VMEM],
        out_shape=[
            jax.ShapeDtypeStruct((my_subs, width, levels), jnp.float32),
            jax.ShapeDtypeStruct((my_subs, levels), jnp.float32),
        ],
        compiler_params=pltpu.CompilerParams(vmem_limit_bytes=8 * MIB),
        name="finish",
    )(core_arg, half, other)
    return new_centroids, table, distortion


def solution(mesh):
    parts = mesh.shape["sub"]
    cores = Mesh(mesh.devices.reshape(-1, CORES, parts), SPLIT)
    in_specs = (
        P(SPLIT, None),
        P(SPLIT),
        P(SPLIT, None),
        P(SPLIT, None),
        P("sub", None, None),
    )
    out_specs = (P(SPLIT, None), P("sub", None, None), P("sub", None))
    return jax.shard_map(
        on_device, mesh=cores, in_specs=in_specs, out_specs=out_specs, check_vma=False
    )
```

```python
import functools

import jax
import jax.numpy as jnp
from jax import lax
from jax.experimental import pallas as pl
from jax.experimental.pallas import tpu as pltpu
from jax.sharding import Mesh, PartitionSpec as P

LANES = 128
COLS = 256
CORES = 2
MIB = 1024 * 1024
IN_VMEM = pl.BlockSpec(memory_space=pltpu.VMEM)
SPLIT = ("chip", "core", "sub")


def split3(x):
    hi = x.astype(jnp.bfloat16)
    rest = x - hi.astype(jnp.float32)
    mid = rest.astype(jnp.bfloat16)
    lo = (rest - mid.astype(jnp.float32)).astype(jnp.bfloat16)
    return hi, mid, lo


def dot(a, b):
    return jnp.dot(a, b, preferred_element_type=jnp.float32)


def pack_kernel(
    lists, pieces, place, v_ref, ids_ref, codes_ref, books_ref, out_ref, old_ref, ids_v, codes_v, sems
):
    rows, dims = v_ref.shape
    subs = codes_ref.shape[0]
    step = rows // pieces
    half = pl.ds(pl.multiple_of(place[1] * LANES, LANES), LANES)
    small = [
        pltpu.make_async_copy(codes_ref, codes_v, sems.at[pieces]),
        pltpu.make_async_copy(ids_ref, ids_v, sems.at[pieces + 1]),
    ]
    moves = [
        pltpu.make_async_copy(
            v_ref.at[pl.ds(i * step, step)],
            out_ref.at[pl.ds(i * step, step), pl.ds(0, dims)],
            sems.at[i],
        )
        for i in range(pieces)
    ]
    moves.append(
        pltpu.make_async_copy(books_ref.at[place[0], :, half], old_ref, sems.at[pieces + 2])
    )
    for move in small + moves:
        move.start()
    for move in small:
        move.wait()
    ids = lax.rem(ids_v[...], lists)
    high = lax.div(ids, 256)
    aux = jnp.concatenate(
        [
            codes_v[...].astype(jnp.float32),
            high.astype(jnp.float32),
            (ids - 256 * high).astype(jnp.float32),
            jnp.zeros((LANES - subs - 2, rows), jnp.float32),
        ],
        axis=0,
    )
    out_ref[:, dims:] = jnp.transpose(aux).astype(jnp.bfloat16)
    for move in moves:
        move.wait()


def pack(place, vectors, list_ids, codes, codebooks, lists):
    rows, dims = vectors.shape
    subs = codes.shape[1]
    width = codebooks.shape[1]
    pieces = 4
    anywhere = pl.BlockSpec(memory_space=pl.ANY)
    sources = (vectors, list_ids.reshape(1, rows), jnp.transpose(codes), codebooks)
    return pl.pallas_call(
        functools.partial(pack_kernel, lists, pieces),
        in_specs=[pl.BlockSpec(memory_space=pltpu.SMEM)] + [anywhere] * 4,
        out_specs=[IN_VMEM, IN_VMEM],
        out_shape=[
            jax.ShapeDtypeStruct((rows, dims + LANES), jnp.bfloat16),
            jax.ShapeDtypeStruct((width, LANES), jnp.float32),
        ],
        scratch_shapes=[
            pltpu.VMEM((1, rows), jnp.int32),
            pltpu.VMEM((subs, rows), jnp.int32),
            pltpu.SemaphoreType.DMA((pieces + 3,)),
        ],
        compiler_params=pltpu.CompilerParams(vmem_limit_bytes=12 * MIB),
        name="pack",
    )(place, *[pltpu.with_memory_space_constraint(x, pltpu.HBM) for x in sources])


def local_kernel(
    subs,
    width,
    parts,
    prior,
    chunk,
    core_ref,
    arr_ref,
    cent_ref,
    nc_ref,
    keep_ref,
    give_ref,
    hot,
    inv,
    code_t,
    table,
    picked,
    low_v,
    high_v,
    norms,
    side_v,
    extra,
    ids_v,
    ids_s,
    nc_v,
    sem,
    nc_sem,
):
    rows = arr_ref.shape[0]
    lists, dims = cent_ref.shape
    tiles = dims // LANES
    here = COLS // width
    group = LANES // width
    side = COLS // LANES
    held = width + 2
    quad = group // 2
    kinds = 4
    first_core = core_ref[0] == 0

    aux = arr_ref[:, dims:]
    aux_t = jnp.transpose(aux.astype(jnp.float32))
    row_ids = (aux_t[subs : subs + 1] * 256.0 + aux_t[subs + 1 : subs + 2]).astype(jnp.int32)
    ids_v[...] = row_ids * tiles
    copy = pltpu.make_async_copy(ids_v, ids_s, sem)
    copy.start()
    level = lax.broadcasted_iota(jnp.int32, (lists, rows), 0)
    hot[...] = jnp.where(level == row_ids, 1.0, 0.0).astype(jnp.bfloat16)
    counts = dot(hot[...], jnp.ones((rows, LANES), jnp.bfloat16))
    inv[...] = 1.0 / (counts + prior)
    for b in range(subs // group):
        block = aux_t[b * group : (b + 1) * group].astype(jnp.int32)
        code_t[b] = jnp.where(block < LANES, block, block - LANES)
    line = lax.broadcasted_iota(jnp.int32, (LANES, LANES), 0)
    lane = lax.broadcasted_iota(jnp.int32, (LANES, LANES), 1)
    twice = jnp.where(line == lax.rem(lane, subs), 1.0, 0.0).astype(jnp.bfloat16)
    both = dot(aux, twice)
    lane = lax.broadcasted_iota(jnp.int32, (rows, LANES), 1)
    inside = jnp.where((both < LANES) == (lane < subs), 1.0, 0.0)
    side_v[:, 3 * LANES :] = inside.astype(jnp.bfloat16)

    totals = dot(hot[...], arr_ref[:, :dims])
    for tile in range(tiles):
        at = slice(tile * LANES, (tile + 1) * LANES)
        old = prior * cent_ref[:, at].astype(jnp.float32)
        nc = (totals[:, at] + old) * inv[...]
        nc_v[:, at] = nc
        table[pl.ds(tile, lists, stride=tiles), :] = nc
    nc_copy = pltpu.make_async_copy(nc_v, nc_ref, nc_sem)
    nc_copy.start()
    copy.wait()

    def pick(q, _):
        for u in range(8):
            r = q * 8 + u
            row = table[pl.ds(pl.multiple_of(ids_s[0, r], 8), tiles), :]
            picked[pl.ds(pl.multiple_of(r * tiles, 8), tiles), :] = row
        return 0

    lax.fori_loop(0, rows // 8, pick, 0, unroll=8)

    def residuals(j, _):
        at = pl.ds(pl.multiple_of(j * COLS, COLS), COLS)
        line = lax.broadcasted_iota(jnp.int32, (LANES, COLS), 0)
        column = lax.broadcasted_iota(jnp.int32, (LANES, COLS), 1)
        widen = jnp.where(line == j * here + column // width, 1.0, 0.0).astype(jnp.bfloat16)
        line = lax.broadcasted_iota(jnp.int32, (COLS, LANES), 0)
        column = lax.broadcasted_iota(jnp.int32, (COLS, LANES), 1)
        fold = jnp.where(
            lax.rem(column, subs) == j * here + line // width, 1.0, 0.0
        ).astype(jnp.bfloat16)
        for i in range(rows // chunk):
            ra = slice(i * chunk, (i + 1) * chunk)
            near = jnp.concatenate(
                [
                    picked[pl.ds(i * chunk * tiles + j * side + h, chunk, stride=tiles), :]
                    for h in range(side)
                ],
                axis=1,
            )
            r = (arr_ref[ra, at].astype(jnp.float32) - near).astype(jnp.bfloat16)
            wide = r.astype(jnp.float32)
            low = r * dot(side_v[ra, 3 * LANES :], widen).astype(jnp.bfloat16)
            low_v[ra, at] = low
            high_v[ra, at] = r - low
            square = wide * wide
            square_hi = square.astype(jnp.bfloat16)
            square_lo = (square - square_hi.astype(jnp.float32)).astype(jnp.bfloat16)
            found = dot(square_hi, fold) + dot(square_lo, fold)
            norms[ra, :] = jnp.where(j == 0, found, norms[ra, :] + found)
        return 0

    lax.fori_loop(0, dims // COLS, residuals, 0, unroll=2)

    for i in range(rows // chunk):
        ra = slice(i * chunk, (i + 1) * chunk)
        pieces = split3(norms[ra, :] * side_v[ra, 3 * LANES :].astype(jnp.float32))
        for k, piece in enumerate(pieces):
            side_v[ra, k * LANES : (k + 1) * LANES] = piece

    def columns(j, _):
        line = lax.broadcasted_iota(jnp.int32, (kinds * LANES, COLS), 0)
        column = lax.broadcasted_iota(jnp.int32, (kinds * LANES, COLS), 1)
        spot = lax.rem(column, LANES // 2)
        in_first = lax.rem(column, LANES) >= LANES // 2
        kind = spot // (2 * quad)
        half = lax.rem(spot, 2 * quad) // quad
        sub = (
            j * here
            + (column // LANES) * group
            + jnp.where(in_first, 0, quad)
            + lax.rem(spot, quad)
        )
        wanted = kind * LANES + half * subs + sub
        move = jnp.where((line == wanted) & (kind < kinds), 1.0, 0.0).astype(jnp.bfloat16)
        for i in range(2 * rows // chunk):
            ra = slice(i * chunk // 2, (i + 1) * chunk // 2)
            extra[ra, :] = dot(side_v[ra, :], move).astype(jnp.bfloat16)

        level = lax.broadcasted_iota(jnp.int32, (LANES, rows), 0)
        level = level.astype(jnp.float32).astype(jnp.bfloat16)
        one = jnp.ones((), jnp.bfloat16)
        zero = jnp.zeros((), jnp.bfloat16)
        lane = lax.broadcasted_iota(jnp.int32, (LANES, LANES), 1)
        wide_lane = lax.broadcasted_iota(jnp.int32, (rows, LANES), 1)
        steps = subs // parts // here
        for part in range(side):
            at = pl.ds(pl.multiple_of(j * COLS + part * LANES, LANES), LANES)
            codes = code_t[j * side + part].astype(jnp.float32).astype(jnp.bfloat16)
            beside = extra[:, part * LANES : (part + 1) * LANES]
            low_sum = jnp.zeros((LANES, LANES), jnp.float32)
            high_sum = low_sum
            extra_sum = low_sum
            for q in range(2):
                own = (wide_lane < LANES // 2) == (q == 0)
                mixed = jnp.where(own, high_v[:, at], beside)
                weights = jnp.concatenate([low_v[:, at], mixed], axis=1)
                apart = (lane >= LANES // 2) == (q == 0)
                onehot = jnp.concatenate(
                    [
                        jnp.where(level == codes[i : i + 1], one, zero)
                        for i in range(q * quad, (q + 1) * quad)
                    ],
                    axis=0,
                )
                every = dot(onehot, weights)
                for k in range(quad):
                    i = q * quad + k
                    found = every[k * LANES : (k + 1) * LANES]
                    low_sum = jnp.where(lane // width == i, found[:, :LANES], low_sum)
                    high_sum = jnp.where(lane // width == i, found[:, LANES:], high_sum)
                    extra_sum = jnp.where(
                        apart & (lax.rem(lane, quad) == k), found[:, LANES:], extra_sum
                    )
            low_t = jnp.transpose(low_sum)
            high_t = jnp.transpose(high_sum)
            extra_t = jnp.transpose(extra_sum)
            for i in range(group):
                q, k = divmod(i, quad)
                base = LANES // 2 if q == 0 else 0
                blocks = []
                for half, sums in ((0, low_t), (1, high_t)):
                    found = [
                        extra_t[row : row + 1]
                        for row in range(base + half * quad + k, base + LANES // 2, 2 * quad)
                    ]
                    norm = (found[0] + found[1]) + found[2]
                    blocks.append(
                        jnp.concatenate(
                            [sums[i * width : (i + 1) * width], found[3], norm], axis=0
                        )
                    )
                sub = lax.rem(j, steps) * here + part * group + i
                at_row = (sub * parts + lax.div(j, steps)) * held
                keep_ref[pl.ds(at_row, held), :] = jnp.where(first_core, blocks[0], blocks[1])
                give_ref[pl.ds(at_row, held), :] = jnp.where(first_core, blocks[1], blocks[0])
        return 0

    for j in range(dims // COLS):
        columns(j, 0)
    nc_copy.wait()


def local_pass(core, arrived, centroids, subs, width, prior, parts):
    rows = arrived.shape[0]
    lists, dims = centroids.shape
    tiles = dims // LANES
    group = LANES // width
    sums = jax.ShapeDtypeStruct((subs * (width + 2), LANES), jnp.float32)
    return pl.pallas_call(
        functools.partial(local_kernel, subs, width, parts, prior, 256),
        in_specs=[pl.BlockSpec(memory_space=pltpu.SMEM), IN_VMEM, IN_VMEM],
        out_specs=[pl.BlockSpec(memory_space=pl.ANY), IN_VMEM, IN_VMEM],
        out_shape=[jax.ShapeDtypeStruct((lists, dims), jnp.float32), sums, sums],
        scratch_shapes=[
            pltpu.VMEM((lists, rows), jnp.bfloat16),
            pltpu.VMEM((lists, LANES), jnp.float32),
            pltpu.VMEM((subs // group, group, rows), jnp.int32),
            pltpu.VMEM((lists * tiles, LANES), jnp.float32),
            pltpu.VMEM((rows * tiles, LANES), jnp.float32),
            pltpu.VMEM((rows, dims), jnp.bfloat16),
            pltpu.VMEM((rows, dims), jnp.bfloat16),
            pltpu.VMEM((rows, LANES), jnp.float32),
            pltpu.VMEM((rows, 4 * LANES), jnp.bfloat16),
            pltpu.VMEM((rows, COLS), jnp.bfloat16),
            pltpu.VMEM((1, rows), jnp.int32),
            pltpu.SMEM((1, rows), jnp.int32),
            pltpu.VMEM((lists, dims), jnp.float32),
            pltpu.SemaphoreType.DMA,
            pltpu.SemaphoreType.DMA,
        ],
        compiler_params=pltpu.CompilerParams(vmem_limit_bytes=32 * MIB),
        name="local_pass",
    )(core, arrived, centroids)


def owner_kernel(width, prior, copies, part_ref, old_ref, out_ref):
    held = width + 2
    sources = part_ref.shape[0] // held
    taken = [part_ref[pl.ds(i, sources, stride=held), :] for i in range(held)]
    sums, counts, norms = taken[:width], taken[width], taken[width + 1]
    count = jnp.sum(counts, axis=0, keepdims=True)
    share = 1.0 / jnp.maximum(counts, 1.0)
    inner = norms
    outer = jnp.zeros_like(norms)
    rows = []
    for d in range(width):
        total = jnp.sum(sums[d], axis=0, keepdims=True)
        new = (total + prior * old_ref[d : d + 1]) / (count + prior)
        mean = sums[d] * share
        gap = mean - new
        inner = inner - sums[d] * mean
        outer = outer + gap * gap
        rows.append(new)
    errors = jnp.sum(jnp.maximum(inner, 0.0) + counts * outer, axis=0, keepdims=True)
    rows.append(errors / (count + 1.0))
    result = jnp.concatenate(rows, axis=0)
    for c in range(copies):
        out_ref[c * (width + 1) : (c + 1) * (width + 1)] = result


def finish_kernel(width, core_ref, mine_ref, other_ref, table_ref, dist_ref):
    held = width + 1
    subs = table_ref.shape[0]
    first_core = core_ref[0] == 0
    for ref, at in ((0, slice(0, LANES)), (1, slice(LANES, 2 * LANES))):
        own = first_core if ref == 0 else jnp.logical_not(first_core)
        for m in range(subs):
            rows = slice(m * held, m * held + width)
            table_ref[m, :, at] = jnp.where(own, mine_ref[rows], other_ref[rows])
        last = pl.ds(width, subs, stride=held)
        dist_ref[:, at] = jnp.where(own, mine_ref[last, :], other_ref[last, :])


def on_device(vectors, list_ids, codes, centroids, codebooks):
    rows, dims = vectors.shape
    chips = lax.axis_size("chip")
    parts = lax.axis_size("sub")
    owners = chips * CORES * parts
    lists = centroids.shape[0]
    subs = codes.shape[1]
    my_subs, width, levels = codebooks.shape
    prior_lists = float(rows // lists)
    prior_codes = float(rows * owners // levels)
    core = lax.axis_index("core")
    core_arg = core.astype(jnp.int32).reshape(1)
    swap = [(0, 1), (1, 0)]

    place = jnp.stack([lax.axis_index("chip"), core]).astype(jnp.int32)
    sent, old = pack(place, vectors, list_ids, codes, codebooks, lists)
    arrived = lax.all_to_all(sent, SPLIT, split_axis=0, concat_axis=0, tiled=True)
    new_centroids, keep, give = local_pass(
        core_arg, arrived, centroids, subs, width, prior_lists, parts
    )
    paired = keep + lax.ppermute(give, "core", swap)
    held = width + 2
    mine = lax.all_to_all(
        paired.reshape(chips * parts, 1, held * LANES),
        ("chip", "sub"),
        split_axis=0,
        concat_axis=0,
        tiled=True,
    ).reshape(chips * parts * held, LANES)
    held = width + 1
    done = pl.pallas_call(
        functools.partial(owner_kernel, width, prior_codes, chips),
        in_specs=[IN_VMEM, IN_VMEM],
        out_specs=IN_VMEM,
        out_shape=jax.ShapeDtypeStruct((chips * held, LANES), jnp.float32),
        compiler_params=pltpu.CompilerParams(vmem_limit_bytes=8 * MIB),
        name="owner_pass",
    )(mine, old)
    half = lax.all_to_all(
        done.reshape(chips, 1, held * LANES), "chip", split_axis=0, concat_axis=0, tiled=True
    ).reshape(chips * held, LANES)
    other = lax.ppermute(half, "core", swap)
    table, distortion = pl.pallas_call(
        functools.partial(finish_kernel, width),
        in_specs=[pl.BlockSpec(memory_space=pltpu.SMEM), IN_VMEM, IN_VMEM],
        out_specs=[IN_VMEM, IN_VMEM],
        out_shape=[
            jax.ShapeDtypeStruct((my_subs, width, levels), jnp.float32),
            jax.ShapeDtypeStruct((my_subs, levels), jnp.float32),
        ],
        compiler_params=pltpu.CompilerParams(vmem_limit_bytes=8 * MIB),
        name="finish",
    )(core_arg, half, other)
    return new_centroids, table, distortion


def solution(mesh):
    parts = mesh.shape["sub"]
    cores = Mesh(mesh.devices.reshape(-1, CORES, parts), SPLIT)
    in_specs = (
        P(SPLIT, None),
        P(SPLIT),
        P(SPLIT, None),
        P(SPLIT, None),
        P("sub", None, None),
    )
    out_specs = (P(SPLIT, None), P("sub", None, None), P("sub", None))
    return jax.shard_map(
        on_device, mesh=cores, in_specs=in_specs, out_specs=out_specs, check_vma=False
    )
```

```python
import functools

import jax
import jax.numpy as jnp
from jax import lax
from jax.experimental import pallas as pl
from jax.experimental.pallas import tpu as pltpu
from jax.sharding import Mesh, PartitionSpec as P

LANES = 128
COLS = 256
CORES = 2
MIB = 1024 * 1024
IN_VMEM = pl.BlockSpec(memory_space=pltpu.VMEM)
FAR = 2
SPLIT = ("far", "plane", "core", "sub")
CHIP = ("far", "plane")
ROW_ORDER = ("plane", "core", "far", "sub")
SUM_ORDER = ("sub", "plane", "far")


def split3(x):
    hi = x.astype(jnp.bfloat16)
    rest = x - hi.astype(jnp.float32)
    mid = rest.astype(jnp.bfloat16)
    lo = (rest - mid.astype(jnp.float32)).astype(jnp.bfloat16)
    return hi, mid, lo


def dot(a, b):
    return jnp.dot(a, b, preferred_element_type=jnp.float32)


def pack_kernel(
    lists, pieces, place, v_ref, ids_ref, codes_ref, books_ref, out_ref, old_ref, ids_v, codes_v, sems
):
    far, runs, run, dims = v_ref.shape
    subs, rows = codes_ref.shape
    step = runs // pieces
    half = pl.ds(pl.multiple_of(place[1] * LANES, LANES), LANES)
    small = [
        pltpu.make_async_copy(codes_ref, codes_v, sems.at[far * pieces]),
        pltpu.make_async_copy(ids_ref, ids_v, sems.at[far * pieces + 1]),
    ]
    moves = [
        pltpu.make_async_copy(
            v_ref.at[f, pl.ds(i * step, step)],
            out_ref.at[pl.ds(i * step, step), f, :, pl.ds(0, dims)],
            sems.at[f * pieces + i],
        )
        for f in range(far)
        for i in range(pieces)
    ]
    moves.append(
        pltpu.make_async_copy(books_ref.at[place[0], :, half], old_ref, sems.at[far * pieces + 2])
    )
    for move in small + moves:
        move.start()
    for move in small:
        move.wait()
    ids = lax.rem(ids_v[...], lists)
    high = lax.div(ids, 256)
    aux = jnp.concatenate(
        [
            codes_v[...].astype(jnp.float32),
            high.astype(jnp.float32),
            (ids - 256 * high).astype(jnp.float32),
            jnp.zeros((LANES - subs - 2, rows), jnp.float32),
        ],
        axis=0,
    )
    aux = jnp.transpose(aux).astype(jnp.bfloat16).reshape(far, runs, run, LANES)
    for f in range(far):
        out_ref[:, f, :, dims:] = aux[f]
    for move in moves:
        move.wait()


def pack(place, vectors, list_ids, codes, codebooks, lists, run):
    rows, dims = vectors.shape
    subs = codes.shape[1]
    width = codebooks.shape[1]
    pieces = 2
    runs = rows // (FAR * run)
    anywhere = pl.BlockSpec(memory_space=pl.ANY)
    sources = (
        vectors.reshape(FAR, runs, run, dims),
        list_ids.reshape(1, rows),
        jnp.transpose(codes),
        codebooks,
    )
    sent, old = pl.pallas_call(
        functools.partial(pack_kernel, lists, pieces),
        in_specs=[pl.BlockSpec(memory_space=pltpu.SMEM)] + [anywhere] * 4,
        out_specs=[IN_VMEM, IN_VMEM],
        out_shape=[
            jax.ShapeDtypeStruct((runs, FAR, run, dims + LANES), jnp.bfloat16),
            jax.ShapeDtypeStruct((width, LANES), jnp.float32),
        ],
        scratch_shapes=[
            pltpu.VMEM((1, rows), jnp.int32),
            pltpu.VMEM((subs, rows), jnp.int32),
            pltpu.SemaphoreType.DMA((FAR * pieces + 3,)),
        ],
        compiler_params=pltpu.CompilerParams(vmem_limit_bytes=12 * MIB),
        name="pack",
    )(place, *[pltpu.with_memory_space_constraint(x, pltpu.HBM) for x in sources])
    return sent.reshape(rows, dims + LANES), old


def local_kernel(
    subs,
    width,
    parts,
    prior,
    chunk,
    core_ref,
    arr_ref,
    cent_ref,
    nc_ref,
    keep_ref,
    give_ref,
    hot,
    inv,
    code_t,
    table,
    picked,
    low_v,
    high_v,
    norms,
    side_v,
    extra,
    ids_v,
    ids_s,
    nc_v,
    sem,
    nc_sem,
):
    rows = arr_ref.shape[0]
    lists, dims = cent_ref.shape
    tiles = dims // LANES
    here = COLS // width
    group = LANES // width
    side = COLS // LANES
    held = width + 2
    quad = group // 2
    kinds = 4
    first_core = core_ref[0] == 0

    aux = arr_ref[:, dims:]
    aux_t = jnp.transpose(aux.astype(jnp.float32))
    row_ids = (aux_t[subs : subs + 1] * 256.0 + aux_t[subs + 1 : subs + 2]).astype(jnp.int32)
    ids_v[...] = row_ids * tiles
    copy = pltpu.make_async_copy(ids_v, ids_s, sem)
    copy.start()
    level = lax.broadcasted_iota(jnp.int32, (lists, rows), 0)
    hot[...] = jnp.where(level == row_ids, 1.0, 0.0).astype(jnp.bfloat16)
    counts = dot(hot[...], jnp.ones((rows, LANES), jnp.bfloat16))
    inv[...] = 1.0 / (counts + prior)
    for b in range(subs // group):
        block = aux_t[b * group : (b + 1) * group].astype(jnp.int32)
        code_t[b] = jnp.where(block < LANES, block, block - LANES)
    line = lax.broadcasted_iota(jnp.int32, (LANES, LANES), 0)
    lane = lax.broadcasted_iota(jnp.int32, (LANES, LANES), 1)
    twice = jnp.where(line == lax.rem(lane, subs), 1.0, 0.0).astype(jnp.bfloat16)
    both = dot(aux, twice)
    lane = lax.broadcasted_iota(jnp.int32, (rows, LANES), 1)
    inside = jnp.where((both < LANES) == (lane < subs), 1.0, 0.0)
    side_v[:, 3 * LANES :] = inside.astype(jnp.bfloat16)

    totals = dot(hot[...], arr_ref[:, :dims])
    for tile in range(tiles):
        at = slice(tile * LANES, (tile + 1) * LANES)
        old = prior * cent_ref[:, at].astype(jnp.float32)
        nc = (totals[:, at] + old) * inv[...]
        nc_v[:, at] = nc
        table[pl.ds(tile, lists, stride=tiles), :] = nc
    nc_copy = pltpu.make_async_copy(nc_v, nc_ref, nc_sem)
    nc_copy.start()
    copy.wait()

    def pick(q, _):
        for u in range(8):
            r = q * 8 + u
            row = table[pl.ds(pl.multiple_of(ids_s[0, r], 8), tiles), :]
            picked[pl.ds(pl.multiple_of(r * tiles, 8), tiles), :] = row
        return 0

    lax.fori_loop(0, rows // 8, pick, 0, unroll=8)

    def residuals(j, _):
        at = pl.ds(pl.multiple_of(j * COLS, COLS), COLS)
        line = lax.broadcasted_iota(jnp.int32, (LANES, COLS), 0)
        column = lax.broadcasted_iota(jnp.int32, (LANES, COLS), 1)
        widen = jnp.where(line == j * here + column // width, 1.0, 0.0).astype(jnp.bfloat16)
        line = lax.broadcasted_iota(jnp.int32, (COLS, LANES), 0)
        column = lax.broadcasted_iota(jnp.int32, (COLS, LANES), 1)
        fold = jnp.where(
            lax.rem(column, subs) == j * here + line // width, 1.0, 0.0
        ).astype(jnp.bfloat16)
        for i in range(rows // chunk):
            ra = slice(i * chunk, (i + 1) * chunk)
            near = jnp.concatenate(
                [
                    picked[pl.ds(i * chunk * tiles + j * side + h, chunk, stride=tiles), :]
                    for h in range(side)
                ],
                axis=1,
            )
            r = (arr_ref[ra, at].astype(jnp.float32) - near).astype(jnp.bfloat16)
            wide = r.astype(jnp.float32)
            low = r * dot(side_v[ra, 3 * LANES :], widen).astype(jnp.bfloat16)
            low_v[ra, at] = low
            high_v[ra, at] = r - low
            square = wide * wide
            square_hi = square.astype(jnp.bfloat16)
            square_lo = (square - square_hi.astype(jnp.float32)).astype(jnp.bfloat16)
            found = dot(square_hi, fold) + dot(square_lo, fold)
            norms[ra, :] = jnp.where(j == 0, found, norms[ra, :] + found)
        return 0

    lax.fori_loop(0, dims // COLS, residuals, 0, unroll=2)

    for i in range(rows // chunk):
        ra = slice(i * chunk, (i + 1) * chunk)
        pieces = split3(norms[ra, :] * side_v[ra, 3 * LANES :].astype(jnp.float32))
        for k, piece in enumerate(pieces):
            side_v[ra, k * LANES : (k + 1) * LANES] = piece

    def columns(j, _):
        line = lax.broadcasted_iota(jnp.int32, (kinds * LANES, COLS), 0)
        column = lax.broadcasted_iota(jnp.int32, (kinds * LANES, COLS), 1)
        spot = lax.rem(column, LANES // 2)
        in_first = lax.rem(column, LANES) >= LANES // 2
        kind = spot // (2 * quad)
        half = lax.rem(spot, 2 * quad) // quad
        sub = (
            j * here
            + (column // LANES) * group
            + jnp.where(in_first, 0, quad)
            + lax.rem(spot, quad)
        )
        wanted = kind * LANES + half * subs + sub
        move = jnp.where((line == wanted) & (kind < kinds), 1.0, 0.0).astype(jnp.bfloat16)
        for i in range(2 * rows // chunk):
            ra = slice(i * chunk // 2, (i + 1) * chunk // 2)
            extra[ra, :] = dot(side_v[ra, :], move).astype(jnp.bfloat16)

        level = lax.broadcasted_iota(jnp.int32, (LANES, rows), 0)
        level = level.astype(jnp.float32).astype(jnp.bfloat16)
        one = jnp.ones((), jnp.bfloat16)
        zero = jnp.zeros((), jnp.bfloat16)
        lane = lax.broadcasted_iota(jnp.int32, (LANES, LANES), 1)
        wide_lane = lax.broadcasted_iota(jnp.int32, (rows, LANES), 1)
        steps = subs // parts // here
        for part in range(side):
            at = pl.ds(pl.multiple_of(j * COLS + part * LANES, LANES), LANES)
            codes = code_t[j * side + part].astype(jnp.float32).astype(jnp.bfloat16)
            beside = extra[:, part * LANES : (part + 1) * LANES]
            low_sum = jnp.zeros((LANES, LANES), jnp.float32)
            high_sum = low_sum
            extra_sum = low_sum
            for q in range(2):
                own = (wide_lane < LANES // 2) == (q == 0)
                mixed = jnp.where(own, high_v[:, at], beside)
                weights = jnp.concatenate([low_v[:, at], mixed], axis=1)
                apart = (lane >= LANES // 2) == (q == 0)
                onehot = jnp.concatenate(
                    [
                        jnp.where(level == codes[i : i + 1], one, zero)
                        for i in range(q * quad, (q + 1) * quad)
                    ],
                    axis=0,
                )
                every = dot(onehot, weights)
                for k in range(quad):
                    i = q * quad + k
                    found = every[k * LANES : (k + 1) * LANES]
                    low_sum = jnp.where(lane // width == i, found[:, :LANES], low_sum)
                    high_sum = jnp.where(lane // width == i, found[:, LANES:], high_sum)
                    extra_sum = jnp.where(
                        apart & (lax.rem(lane, quad) == k), found[:, LANES:], extra_sum
                    )
            low_t = jnp.transpose(low_sum)
            high_t = jnp.transpose(high_sum)
            extra_t = jnp.transpose(extra_sum)
            for i in range(group):
                q, k = divmod(i, quad)
                base = LANES // 2 if q == 0 else 0
                blocks = []
                for half, sums in ((0, low_t), (1, high_t)):
                    found = [
                        extra_t[row : row + 1]
                        for row in range(base + half * quad + k, base + LANES // 2, 2 * quad)
                    ]
                    norm = (found[0] + found[1]) + found[2]
                    blocks.append(
                        jnp.concatenate(
                            [sums[i * width : (i + 1) * width], found[3], norm], axis=0
                        )
                    )
                sub = (j % steps) * here + part * group + i
                near = subs // parts // FAR
                at_row = ((j // steps * near + sub % near) * FAR + sub // near) * held
                keep_ref[pl.ds(at_row, held), :] = jnp.where(first_core, blocks[0], blocks[1])
                give_ref[pl.ds(at_row, held), :] = jnp.where(first_core, blocks[1], blocks[0])
        return 0

    for j in range(dims // COLS):
        columns(j, 0)
    nc_copy.wait()


def local_pass(core, arrived, centroids, subs, width, prior, parts):
    rows = arrived.shape[0]
    lists, dims = centroids.shape
    tiles = dims // LANES
    group = LANES // width
    sums = jax.ShapeDtypeStruct((subs * (width + 2), LANES), jnp.float32)
    return pl.pallas_call(
        functools.partial(local_kernel, subs, width, parts, prior, 256),
        in_specs=[pl.BlockSpec(memory_space=pltpu.SMEM), IN_VMEM, IN_VMEM],
        out_specs=[pl.BlockSpec(memory_space=pl.ANY), IN_VMEM, IN_VMEM],
        out_shape=[jax.ShapeDtypeStruct((lists, dims), jnp.float32), sums, sums],
        scratch_shapes=[
            pltpu.VMEM((lists, rows), jnp.bfloat16),
            pltpu.VMEM((lists, LANES), jnp.float32),
            pltpu.VMEM((subs // group, group, rows), jnp.int32),
            pltpu.VMEM((lists * tiles, LANES), jnp.float32),
            pltpu.VMEM((rows * tiles, LANES), jnp.float32),
            pltpu.VMEM((rows, dims), jnp.bfloat16),
            pltpu.VMEM((rows, dims), jnp.bfloat16),
            pltpu.VMEM((rows, LANES), jnp.float32),
            pltpu.VMEM((rows, 4 * LANES), jnp.bfloat16),
            pltpu.VMEM((rows, COLS), jnp.bfloat16),
            pltpu.VMEM((1, rows), jnp.int32),
            pltpu.SMEM((1, rows), jnp.int32),
            pltpu.VMEM((lists, dims), jnp.float32),
            pltpu.SemaphoreType.DMA,
            pltpu.SemaphoreType.DMA,
        ],
        compiler_params=pltpu.CompilerParams(vmem_limit_bytes=32 * MIB),
        name="local_pass",
    )(core, arrived, centroids)


def owner_kernel(width, prior, copies, part_ref, old_ref, out_ref):
    held = width + 2
    sources = part_ref.shape[0] // held
    taken = [part_ref[pl.ds(i, sources, stride=held), :] for i in range(held)]
    sums, counts, norms = taken[:width], taken[width], taken[width + 1]
    count = jnp.sum(counts, axis=0, keepdims=True)
    share = 1.0 / jnp.maximum(counts, 1.0)
    inner = norms
    outer = jnp.zeros_like(norms)
    rows = []
    for d in range(width):
        total = jnp.sum(sums[d], axis=0, keepdims=True)
        new = (total + prior * old_ref[d : d + 1]) / (count + prior)
        mean = sums[d] * share
        gap = mean - new
        inner = inner - sums[d] * mean
        outer = outer + gap * gap
        rows.append(new)
    errors = jnp.sum(jnp.maximum(inner, 0.0) + counts * outer, axis=0, keepdims=True)
    rows.append(errors / (count + 1.0))
    result = jnp.concatenate(rows, axis=0)
    for c in range(copies):
        out_ref[c * (width + 1) : (c + 1) * (width + 1)] = result


def finish_kernel(width, core_ref, mine_ref, other_ref, table_ref, dist_ref):
    held = width + 1
    subs = table_ref.shape[0]
    first_core = core_ref[0] == 0
    for ref, at in ((0, slice(0, LANES)), (1, slice(LANES, 2 * LANES))):
        own = first_core if ref == 0 else jnp.logical_not(first_core)
        for m in range(subs):
            rows = slice(m * held, m * held + width)
            table_ref[m, :, at] = jnp.where(own, mine_ref[rows], other_ref[rows])
        last = pl.ds(width, subs, stride=held)
        dist_ref[:, at] = jnp.where(own, mine_ref[last, :], other_ref[last, :])


def on_device(vectors, list_ids, codes, centroids, codebooks):
    rows, dims = vectors.shape
    chips = lax.axis_size("far") * lax.axis_size("plane")
    parts = lax.axis_size("sub")
    owners = chips * CORES * parts
    lists = centroids.shape[0]
    subs = codes.shape[1]
    my_subs, width, levels = codebooks.shape
    prior_lists = float(rows // lists)
    prior_codes = float(rows * owners // levels)
    core = lax.axis_index("core")
    core_arg = core.astype(jnp.int32).reshape(1)
    swap = [(0, 1), (1, 0)]

    place = jnp.stack([lax.axis_index(CHIP), core]).astype(jnp.int32)
    run = rows // (chips * CORES)
    sent, old = pack(place, vectors, list_ids, codes, codebooks, lists, run)
    arrived = lax.all_to_all(sent, ROW_ORDER, split_axis=0, concat_axis=0, tiled=True)
    new_centroids, keep, give = local_pass(
        core_arg, arrived, centroids, subs, width, prior_lists, parts
    )
    paired = keep + lax.ppermute(give, "core", swap)
    held = width + 2
    mine = lax.all_to_all(
        paired.reshape(chips * parts, 1, held * LANES),
        SUM_ORDER,
        split_axis=0,
        concat_axis=0,
        tiled=True,
    ).reshape(chips * parts * held, LANES)
    held = width + 1
    done = pl.pallas_call(
        functools.partial(owner_kernel, width, prior_codes, chips),
        in_specs=[IN_VMEM, IN_VMEM],
        out_specs=IN_VMEM,
        out_shape=jax.ShapeDtypeStruct((chips * held, LANES), jnp.float32),
        compiler_params=pltpu.CompilerParams(vmem_limit_bytes=8 * MIB),
        name="owner_pass",
    )(mine, old)
    half = lax.all_to_all(
        done.reshape(chips, 1, held * LANES), CHIP, split_axis=0, concat_axis=0, tiled=True
    ).reshape(chips * held, LANES)
    other = lax.ppermute(half, "core", swap)
    table, distortion = pl.pallas_call(
        functools.partial(finish_kernel, width),
        in_specs=[pl.BlockSpec(memory_space=pltpu.SMEM), IN_VMEM, IN_VMEM],
        out_specs=[IN_VMEM, IN_VMEM],
        out_shape=[
            jax.ShapeDtypeStruct((my_subs, width, levels), jnp.float32),
            jax.ShapeDtypeStruct((my_subs, levels), jnp.float32),
        ],
        compiler_params=pltpu.CompilerParams(vmem_limit_bytes=8 * MIB),
        name="finish",
    )(core_arg, half, other)
    return new_centroids, table, distortion


def solution(mesh):
    parts = mesh.shape["sub"]
    cores = Mesh(mesh.devices.reshape(FAR, -1, CORES, parts), SPLIT)
    in_specs = (
        P(SPLIT, None),
        P(SPLIT),
        P(SPLIT, None),
        P(SPLIT, None),
        P("sub", None, None),
    )
    out_specs = (P(SPLIT, None), P("sub", None, None), P("sub", None))
    return jax.shard_map(
        on_device, mesh=cores, in_specs=in_specs, out_specs=out_specs, check_vma=False
    )
```

```python
import functools

import jax
import jax.numpy as jnp
from jax import lax
from jax.experimental import pallas as pl
from jax.experimental.pallas import tpu as pltpu
from jax.sharding import Mesh, PartitionSpec as P

LANES = 128
COLS = 256
CORES = 2
MIB = 1024 * 1024
IN_VMEM = pl.BlockSpec(memory_space=pltpu.VMEM)
FAR = 2
DEEP = 4
SPLIT = ("far", "y", "z", "core", "sub")
CHIP = ("far", "y", "z")
ROW_ORDER = ("far", "z", "core", "y", "sub")
SUM_ORDER = ("sub", "y", "z", "far")
RESULT_ORDER = ("far", "z", "y")


def split3(x):
    hi = x.astype(jnp.bfloat16)
    rest = x - hi.astype(jnp.float32)
    mid = rest.astype(jnp.bfloat16)
    lo = (rest - mid.astype(jnp.float32)).astype(jnp.bfloat16)
    return hi, mid, lo


def dot(a, b):
    return jnp.dot(a, b, preferred_element_type=jnp.float32)


def pack_kernel(
    lists, place, v_ref, ids_ref, codes_ref, books_ref, out_ref, old_ref, ids_v, codes_v, sems
):
    far, deep, runs, run, dims = v_ref.shape
    subs, rows = codes_ref.shape
    pieces = far * deep
    half = pl.ds(pl.multiple_of(place[1] * LANES, LANES), LANES)
    small = [
        pltpu.make_async_copy(codes_ref, codes_v, sems.at[pieces]),
        pltpu.make_async_copy(ids_ref, ids_v, sems.at[pieces + 1]),
    ]
    moves = [
        pltpu.make_async_copy(
            v_ref.at[f, y],
            out_ref.at[f, :, y, :, pl.ds(0, dims)],
            sems.at[f * deep + y],
        )
        for f in range(far)
        for y in range(deep)
    ]
    moves.append(
        pltpu.make_async_copy(books_ref.at[place[0], :, half], old_ref, sems.at[pieces + 2])
    )
    for move in small + moves:
        move.start()
    for move in small:
        move.wait()
    ids = lax.rem(ids_v[...], lists)
    high = lax.div(ids, 256)
    aux = jnp.concatenate(
        [
            codes_v[...].astype(jnp.float32),
            high.astype(jnp.float32),
            (ids - 256 * high).astype(jnp.float32),
            jnp.zeros((LANES - subs - 2, rows), jnp.float32),
        ],
        axis=0,
    )
    aux = jnp.transpose(aux).astype(jnp.bfloat16).reshape(far, deep, runs, run, LANES)
    for f in range(far):
        for y in range(deep):
            out_ref[f, :, y, :, dims:] = aux[f, y]
    for move in moves:
        move.wait()


def pack(place, vectors, list_ids, codes, codebooks, lists, run):
    rows, dims = vectors.shape
    subs = codes.shape[1]
    width = codebooks.shape[1]
    runs = rows // (FAR * DEEP * run)
    anywhere = pl.BlockSpec(memory_space=pl.ANY)
    sources = (
        vectors.reshape(FAR, DEEP, runs, run, dims),
        list_ids.reshape(1, rows),
        jnp.transpose(codes),
        codebooks,
    )
    sent, old = pl.pallas_call(
        functools.partial(pack_kernel, lists),
        in_specs=[pl.BlockSpec(memory_space=pltpu.SMEM)] + [anywhere] * 4,
        out_specs=[IN_VMEM, IN_VMEM],
        out_shape=[
            jax.ShapeDtypeStruct((FAR, runs, DEEP, run, dims + LANES), jnp.bfloat16),
            jax.ShapeDtypeStruct((width, LANES), jnp.float32),
        ],
        scratch_shapes=[
            pltpu.VMEM((1, rows), jnp.int32),
            pltpu.VMEM((subs, rows), jnp.int32),
            pltpu.SemaphoreType.DMA((FAR * DEEP + 3,)),
        ],
        compiler_params=pltpu.CompilerParams(vmem_limit_bytes=12 * MIB),
        name="pack",
    )(place, *[pltpu.with_memory_space_constraint(x, pltpu.HBM) for x in sources])
    return sent.reshape(rows, dims + LANES), old


def local_kernel(
    subs,
    width,
    parts,
    prior,
    chunk,
    core_ref,
    arr_ref,
    cent_ref,
    nc_ref,
    keep_ref,
    give_ref,
    hot,
    inv,
    code_t,
    table,
    picked,
    low_v,
    high_v,
    norms,
    side_v,
    extra,
    ids_v,
    ids_s,
    nc_v,
    sem,
    nc_sem,
):
    rows = arr_ref.shape[0]
    lists, dims = cent_ref.shape
    tiles = dims // LANES
    here = COLS // width
    group = LANES // width
    side = COLS // LANES
    held = width + 2
    quad = group // 2
    kinds = 4
    first_core = core_ref[0] == 0

    aux = arr_ref[:, dims:]
    aux_t = jnp.transpose(aux.astype(jnp.float32))
    row_ids = (aux_t[subs : subs + 1] * 256.0 + aux_t[subs + 1 : subs + 2]).astype(jnp.int32)
    ids_v[...] = row_ids * tiles
    copy = pltpu.make_async_copy(ids_v, ids_s, sem)
    copy.start()
    level = lax.broadcasted_iota(jnp.int32, (lists, rows), 0)
    hot[...] = jnp.where(level == row_ids, 1.0, 0.0).astype(jnp.bfloat16)
    counts = dot(hot[...], jnp.ones((rows, LANES), jnp.bfloat16))
    inv[...] = 1.0 / (counts + prior)
    for b in range(subs // group):
        block = aux_t[b * group : (b + 1) * group].astype(jnp.int32)
        code_t[b] = jnp.where(block < LANES, block, block - LANES)
    line = lax.broadcasted_iota(jnp.int32, (LANES, LANES), 0)
    lane = lax.broadcasted_iota(jnp.int32, (LANES, LANES), 1)
    twice = jnp.where(line == lax.rem(lane, subs), 1.0, 0.0).astype(jnp.bfloat16)
    both = dot(aux, twice)
    lane = lax.broadcasted_iota(jnp.int32, (rows, LANES), 1)
    inside = jnp.where((both < LANES) == (lane < subs), 1.0, 0.0)
    side_v[:, 3 * LANES :] = inside.astype(jnp.bfloat16)

    totals = dot(hot[...], arr_ref[:, :dims])
    for tile in range(tiles):
        at = slice(tile * LANES, (tile + 1) * LANES)
        old = prior * cent_ref[:, at].astype(jnp.float32)
        nc = (totals[:, at] + old) * inv[...]
        nc_v[:, at] = nc
        table[pl.ds(tile, lists, stride=tiles), :] = nc
    nc_copy = pltpu.make_async_copy(nc_v, nc_ref, nc_sem)
    nc_copy.start()
    copy.wait()

    def pick(q, _):
        for u in range(8):
            r = q * 8 + u
            row = table[pl.ds(pl.multiple_of(ids_s[0, r], 8), tiles), :]
            picked[pl.ds(pl.multiple_of(r * tiles, 8), tiles), :] = row
        return 0

    lax.fori_loop(0, rows // 8, pick, 0, unroll=8)

    def residuals(j, _):
        at = pl.ds(pl.multiple_of(j * COLS, COLS), COLS)
        line = lax.broadcasted_iota(jnp.int32, (LANES, COLS), 0)
        column = lax.broadcasted_iota(jnp.int32, (LANES, COLS), 1)
        widen = jnp.where(line == j * here + column // width, 1.0, 0.0).astype(jnp.bfloat16)
        line = lax.broadcasted_iota(jnp.int32, (COLS, LANES), 0)
        column = lax.broadcasted_iota(jnp.int32, (COLS, LANES), 1)
        fold = jnp.where(
            lax.rem(column, subs) == j * here + line // width, 1.0, 0.0
        ).astype(jnp.bfloat16)
        for i in range(rows // chunk):
            ra = slice(i * chunk, (i + 1) * chunk)
            near = jnp.concatenate(
                [
                    picked[pl.ds(i * chunk * tiles + j * side + h, chunk, stride=tiles), :]
                    for h in range(side)
                ],
                axis=1,
            )
            r = (arr_ref[ra, at].astype(jnp.float32) - near).astype(jnp.bfloat16)
            wide = r.astype(jnp.float32)
            low = r * dot(side_v[ra, 3 * LANES :], widen).astype(jnp.bfloat16)
            low_v[ra, at] = low
            high_v[ra, at] = r - low
            square = wide * wide
            square_hi = square.astype(jnp.bfloat16)
            square_lo = (square - square_hi.astype(jnp.float32)).astype(jnp.bfloat16)
            found = dot(square_hi, fold) + dot(square_lo, fold)
            norms[ra, :] = jnp.where(j == 0, found, norms[ra, :] + found)
        return 0

    lax.fori_loop(0, dims // COLS, residuals, 0, unroll=2)

    for i in range(rows // chunk):
        ra = slice(i * chunk, (i + 1) * chunk)
        pieces = split3(norms[ra, :] * side_v[ra, 3 * LANES :].astype(jnp.float32))
        for k, piece in enumerate(pieces):
            side_v[ra, k * LANES : (k + 1) * LANES] = piece

    def columns(j, _):
        line = lax.broadcasted_iota(jnp.int32, (kinds * LANES, COLS), 0)
        column = lax.broadcasted_iota(jnp.int32, (kinds * LANES, COLS), 1)
        spot = lax.rem(column, LANES // 2)
        in_first = lax.rem(column, LANES) >= LANES // 2
        kind = spot // (2 * quad)
        half = lax.rem(spot, 2 * quad) // quad
        sub = (
            j * here
            + (column // LANES) * group
            + jnp.where(in_first, 0, quad)
            + lax.rem(spot, quad)
        )
        wanted = kind * LANES + half * subs + sub
        move = jnp.where((line == wanted) & (kind < kinds), 1.0, 0.0).astype(jnp.bfloat16)
        for i in range(2 * rows // chunk):
            ra = slice(i * chunk // 2, (i + 1) * chunk // 2)
            extra[ra, :] = dot(side_v[ra, :], move).astype(jnp.bfloat16)

        level = lax.broadcasted_iota(jnp.int32, (LANES, rows), 0)
        level = level.astype(jnp.float32).astype(jnp.bfloat16)
        one = jnp.ones((), jnp.bfloat16)
        zero = jnp.zeros((), jnp.bfloat16)
        lane = lax.broadcasted_iota(jnp.int32, (LANES, LANES), 1)
        wide_lane = lax.broadcasted_iota(jnp.int32, (rows, LANES), 1)
        steps = subs // parts // here
        for part in range(side):
            at = pl.ds(pl.multiple_of(j * COLS + part * LANES, LANES), LANES)
            codes = code_t[j * side + part].astype(jnp.float32).astype(jnp.bfloat16)
            beside = extra[:, part * LANES : (part + 1) * LANES]
            low_sum = jnp.zeros((LANES, LANES), jnp.float32)
            high_sum = low_sum
            extra_sum = low_sum
            for q in range(2):
                own = (wide_lane < LANES // 2) == (q == 0)
                mixed = jnp.where(own, high_v[:, at], beside)
                weights = jnp.concatenate([low_v[:, at], mixed], axis=1)
                apart = (lane >= LANES // 2) == (q == 0)
                onehot = jnp.concatenate(
                    [
                        jnp.where(level == codes[i : i + 1], one, zero)
                        for i in range(q * quad, (q + 1) * quad)
                    ],
                    axis=0,
                )
                every = dot(onehot, weights)
                for k in range(quad):
                    i = q * quad + k
                    found = every[k * LANES : (k + 1) * LANES]
                    low_sum = jnp.where(lane // width == i, found[:, :LANES], low_sum)
                    high_sum = jnp.where(lane // width == i, found[:, LANES:], high_sum)
                    extra_sum = jnp.where(
                        apart & (lax.rem(lane, quad) == k), found[:, LANES:], extra_sum
                    )
            low_t = jnp.transpose(low_sum)
            high_t = jnp.transpose(high_sum)
            extra_t = jnp.transpose(extra_sum)
            for i in range(group):
                q, k = divmod(i, quad)
                base = LANES // 2 if q == 0 else 0
                blocks = []
                for half, sums in ((0, low_t), (1, high_t)):
                    found = [
                        extra_t[row : row + 1]
                        for row in range(base + half * quad + k, base + LANES // 2, 2 * quad)
                    ]
                    norm = (found[0] + found[1]) + found[2]
                    blocks.append(
                        jnp.concatenate(
                            [sums[i * width : (i + 1) * width], found[3], norm], axis=0
                        )
                    )
                sub = (j % steps) * here + part * group + i
                near = subs // parts // FAR
                at_row = ((j // steps * near + sub % near) * FAR + sub // near) * held
                keep_ref[pl.ds(at_row, held), :] = jnp.where(first_core, blocks[0], blocks[1])
                give_ref[pl.ds(at_row, held), :] = jnp.where(first_core, blocks[1], blocks[0])
        return 0

    for j in range(dims // COLS):
        columns(j, 0)
    nc_copy.wait()


def local_pass(core, arrived, centroids, subs, width, prior, parts):
    rows = arrived.shape[0]
    lists, dims = centroids.shape
    tiles = dims // LANES
    group = LANES // width
    sums = jax.ShapeDtypeStruct((subs * (width + 2), LANES), jnp.float32)
    return pl.pallas_call(
        functools.partial(local_kernel, subs, width, parts, prior, 256),
        in_specs=[pl.BlockSpec(memory_space=pltpu.SMEM), IN_VMEM, IN_VMEM],
        out_specs=[pl.BlockSpec(memory_space=pl.ANY), IN_VMEM, IN_VMEM],
        out_shape=[jax.ShapeDtypeStruct((lists, dims), jnp.float32), sums, sums],
        scratch_shapes=[
            pltpu.VMEM((lists, rows), jnp.bfloat16),
            pltpu.VMEM((lists, LANES), jnp.float32),
            pltpu.VMEM((subs // group, group, rows), jnp.int32),
            pltpu.VMEM((lists * tiles, LANES), jnp.float32),
            pltpu.VMEM((rows * tiles, LANES), jnp.float32),
            pltpu.VMEM((rows, dims), jnp.bfloat16),
            pltpu.VMEM((rows, dims), jnp.bfloat16),
            pltpu.VMEM((rows, LANES), jnp.float32),
            pltpu.VMEM((rows, 4 * LANES), jnp.bfloat16),
            pltpu.VMEM((rows, COLS), jnp.bfloat16),
            pltpu.VMEM((1, rows), jnp.int32),
            pltpu.SMEM((1, rows), jnp.int32),
            pltpu.VMEM((lists, dims), jnp.float32),
            pltpu.SemaphoreType.DMA,
            pltpu.SemaphoreType.DMA,
        ],
        compiler_params=pltpu.CompilerParams(vmem_limit_bytes=32 * MIB),
        name="local_pass",
    )(core, arrived, centroids)


def owner_kernel(width, prior, copies, part_ref, old_ref, out_ref):
    held = width + 2
    sources = part_ref.shape[0] // held
    taken = [part_ref[pl.ds(i, sources, stride=held), :] for i in range(held)]
    sums, counts, norms = taken[:width], taken[width], taken[width + 1]
    count = jnp.sum(counts, axis=0, keepdims=True)
    share = 1.0 / jnp.maximum(counts, 1.0)
    inner = norms
    outer = jnp.zeros_like(norms)
    rows = []
    for d in range(width):
        total = jnp.sum(sums[d], axis=0, keepdims=True)
        new = (total + prior * old_ref[d : d + 1]) / (count + prior)
        mean = sums[d] * share
        gap = mean - new
        inner = inner - sums[d] * mean
        outer = outer + gap * gap
        rows.append(new)
    errors = jnp.sum(jnp.maximum(inner, 0.0) + counts * outer, axis=0, keepdims=True)
    rows.append(errors / (count + 1.0))
    result = jnp.concatenate(rows, axis=0)
    for c in range(copies):
        out_ref[c * (width + 1) : (c + 1) * (width + 1)] = result


def finish_kernel(width, core_ref, mine_ref, other_ref, table_ref, dist_ref):
    held = width + 1
    subs = table_ref.shape[0]
    wide = subs // (FAR * DEEP)
    first_core = core_ref[0] == 0
    for half, at in ((0, slice(0, LANES)), (1, slice(LANES, 2 * LANES))):
        own = first_core if half == 0 else jnp.logical_not(first_core)
        for block in range(FAR * DEEP):
            far, y = divmod(block, DEEP)
            start = (far * wide * DEEP + y) * held
            for z in range(wide):
                rows = slice(start + z * DEEP * held, start + z * DEEP * held + width)
                table_ref[block * wide + z, :, at] = jnp.where(
                    own, mine_ref[rows], other_ref[rows]
                )
            last = pl.ds(start + width, wide, stride=DEEP * held)
            dist_ref[block * wide : (block + 1) * wide, at] = jnp.where(
                own, mine_ref[last, :], other_ref[last, :]
            )


def on_device(vectors, list_ids, codes, centroids, codebooks):
    rows, dims = vectors.shape
    chips = lax.axis_size("far") * lax.axis_size("y") * lax.axis_size("z")
    parts = lax.axis_size("sub")
    owners = chips * CORES * parts
    lists = centroids.shape[0]
    subs = codes.shape[1]
    my_subs, width, levels = codebooks.shape
    prior_lists = float(rows // lists)
    prior_codes = float(rows * owners // levels)
    core = lax.axis_index("core")
    core_arg = core.astype(jnp.int32).reshape(1)
    swap = [(0, 1), (1, 0)]

    place = jnp.stack([lax.axis_index(CHIP), core]).astype(jnp.int32)
    run = rows // (chips * CORES)
    sent, old = pack(place, vectors, list_ids, codes, codebooks, lists, run)
    arrived = lax.all_to_all(sent, ROW_ORDER, split_axis=0, concat_axis=0, tiled=True)
    new_centroids, keep, give = local_pass(
        core_arg, arrived, centroids, subs, width, prior_lists, parts
    )
    paired = keep + lax.ppermute(give, "core", swap)
    held = width + 2
    mine = lax.all_to_all(
        paired.reshape(chips * parts, 1, held * LANES),
        SUM_ORDER,
        split_axis=0,
        concat_axis=0,
        tiled=True,
    ).reshape(chips * parts * held, LANES)
    held = width + 1
    done = pl.pallas_call(
        functools.partial(owner_kernel, width, prior_codes, chips),
        in_specs=[IN_VMEM, IN_VMEM],
        out_specs=IN_VMEM,
        out_shape=jax.ShapeDtypeStruct((chips * held, LANES), jnp.float32),
        compiler_params=pltpu.CompilerParams(vmem_limit_bytes=8 * MIB),
        name="owner_pass",
    )(mine, old)
    half = lax.all_to_all(
        done.reshape(chips, 1, held * LANES), RESULT_ORDER, split_axis=0, concat_axis=0, tiled=True
    ).reshape(chips * held, LANES)
    other = lax.ppermute(half, "core", swap)
    table, distortion = pl.pallas_call(
        functools.partial(finish_kernel, width),
        in_specs=[pl.BlockSpec(memory_space=pltpu.SMEM), IN_VMEM, IN_VMEM],
        out_specs=[IN_VMEM, IN_VMEM],
        out_shape=[
            jax.ShapeDtypeStruct((my_subs, width, levels), jnp.float32),
            jax.ShapeDtypeStruct((my_subs, levels), jnp.float32),
        ],
        compiler_params=pltpu.CompilerParams(vmem_limit_bytes=8 * MIB),
        name="finish",
    )(core_arg, half, other)
    return new_centroids, table, distortion


def solution(mesh):
    parts = mesh.shape["sub"]
    cores = Mesh(mesh.devices.reshape(FAR, DEEP, -1, CORES, parts), SPLIT)
    in_specs = (
        P(SPLIT, None),
        P(SPLIT),
        P(SPLIT, None),
        P(SPLIT, None),
        P("sub", None, None),
    )
    out_specs = (P(SPLIT, None), P("sub", None, None), P("sub", None))
    return jax.shard_map(
        on_device, mesh=cores, in_specs=in_specs, out_specs=out_specs, check_vma=False
    )
```

```python
import functools

import jax
import jax.numpy as jnp
from jax import lax
from jax.experimental import pallas as pl
from jax.experimental.pallas import tpu as pltpu
from jax.sharding import Mesh, PartitionSpec as P

LANES = 128
COLS = 256
CORES = 2
MIB = 1024 * 1024
IN_VMEM = pl.BlockSpec(memory_space=pltpu.VMEM)
FAR = 2
SPLIT = ("far", "plane", "core", "sub")
CHIP = ("far", "plane")
ROW_ORDER = ("plane", "core", "far", "sub")
SUM_ORDER = ("sub", "plane", "far")


def split3(x):
    hi = x.astype(jnp.bfloat16)
    rest = x - hi.astype(jnp.float32)
    mid = rest.astype(jnp.bfloat16)
    lo = (rest - mid.astype(jnp.float32)).astype(jnp.bfloat16)
    return hi, mid, lo


def dot(a, b):
    return jnp.dot(a, b, preferred_element_type=jnp.float32)


def pack_kernel(
    lists, pieces, place, v_ref, ids_ref, codes_ref, books_ref, out_ref, old_ref, ids_v, codes_v, sems
):
    far, runs, run, dims = v_ref.shape
    subs, rows = codes_ref.shape
    step = runs // pieces
    half = pl.ds(pl.multiple_of(place[1] * LANES, LANES), LANES)
    small = [
        pltpu.make_async_copy(codes_ref, codes_v, sems.at[far * pieces]),
        pltpu.make_async_copy(ids_ref, ids_v, sems.at[far * pieces + 1]),
    ]
    moves = [
        pltpu.make_async_copy(
            v_ref.at[f, pl.ds(i * step, step)],
            out_ref.at[pl.ds(i * step, step), f, :, pl.ds(0, dims)],
            sems.at[f * pieces + i],
        )
        for f in range(far)
        for i in range(pieces)
    ]
    moves.append(
        pltpu.make_async_copy(books_ref.at[place[0], :, half], old_ref, sems.at[far * pieces + 2])
    )
    for move in small + moves:
        move.start()
    for move in small:
        move.wait()
    ids = lax.rem(ids_v[...], lists)
    high = lax.div(ids, 256)
    aux = jnp.concatenate(
        [
            codes_v[...].astype(jnp.float32),
            high.astype(jnp.float32),
            (ids - 256 * high).astype(jnp.float32),
            jnp.zeros((LANES - subs - 2, rows), jnp.float32),
        ],
        axis=0,
    )
    aux = jnp.transpose(aux).astype(jnp.bfloat16).reshape(far, runs, run, LANES)
    for f in range(far):
        out_ref[:, f, :, dims:] = aux[f]
    for move in moves:
        move.wait()


def pack(place, vectors, list_ids, codes, codebooks, lists, run):
    rows, dims = vectors.shape
    subs = codes.shape[1]
    width = codebooks.shape[1]
    pieces = 2
    runs = rows // (FAR * run)
    anywhere = pl.BlockSpec(memory_space=pl.ANY)
    sources = (
        vectors.reshape(FAR, runs, run, dims),
        list_ids.reshape(1, rows),
        jnp.transpose(codes),
        codebooks,
    )
    sent, old = pl.pallas_call(
        functools.partial(pack_kernel, lists, pieces),
        in_specs=[pl.BlockSpec(memory_space=pltpu.SMEM)] + [anywhere] * 4,
        out_specs=[IN_VMEM, IN_VMEM],
        out_shape=[
            jax.ShapeDtypeStruct((runs, FAR, run, dims + LANES), jnp.bfloat16),
            jax.ShapeDtypeStruct((width, LANES), jnp.float32),
        ],
        scratch_shapes=[
            pltpu.VMEM((1, rows), jnp.int32),
            pltpu.VMEM((subs, rows), jnp.int32),
            pltpu.SemaphoreType.DMA((FAR * pieces + 3,)),
        ],
        compiler_params=pltpu.CompilerParams(vmem_limit_bytes=12 * MIB),
        name="pack",
    )(place, *[pltpu.with_memory_space_constraint(x, pltpu.HBM) for x in sources])
    return sent.reshape(rows, dims + LANES), old


def local_kernel(
    subs,
    width,
    parts,
    prior,
    chunk,
    core_ref,
    arr_ref,
    cent_ref,
    nc_ref,
    keep_ref,
    give_ref,
    hot,
    inv,
    code_t,
    table,
    picked,
    low_v,
    high_v,
    norms,
    side_v,
    extra,
    ids_v,
    ids_s,
    nc_v,
    sem,
    nc_sem,
):
    rows = arr_ref.shape[0]
    lists, dims = cent_ref.shape
    tiles = dims // LANES
    here = COLS // width
    group = LANES // width
    side = COLS // LANES
    held = width + 2
    quad = group // 2
    kinds = 4
    first_core = core_ref[0] == 0

    aux = arr_ref[:, dims:]
    aux_t = jnp.transpose(aux.astype(jnp.float32))
    row_ids = (aux_t[subs : subs + 1] * 256.0 + aux_t[subs + 1 : subs + 2]).astype(jnp.int32)
    ids_v[...] = row_ids * tiles
    copy = pltpu.make_async_copy(ids_v, ids_s, sem)
    copy.start()
    level = lax.broadcasted_iota(jnp.int32, (lists, rows), 0)
    hot[...] = jnp.where(level == row_ids, 1.0, 0.0).astype(jnp.bfloat16)
    counts = dot(hot[...], jnp.ones((rows, LANES), jnp.bfloat16))
    inv[...] = 1.0 / (counts + prior)
    for b in range(subs // group):
        block = aux_t[b * group : (b + 1) * group].astype(jnp.int32)
        code_t[b] = jnp.where(block < LANES, block, block - LANES)
    line = lax.broadcasted_iota(jnp.int32, (LANES, LANES), 0)
    lane = lax.broadcasted_iota(jnp.int32, (LANES, LANES), 1)
    twice = jnp.where(line == lax.rem(lane, subs), 1.0, 0.0).astype(jnp.bfloat16)
    both = dot(aux, twice)
    lane = lax.broadcasted_iota(jnp.int32, (rows, LANES), 1)
    inside = jnp.where((both < LANES) == (lane < subs), 1.0, 0.0)
    side_v[:, 3 * LANES :] = inside.astype(jnp.bfloat16)

    totals = dot(hot[...], arr_ref[:, :dims])
    for tile in range(tiles):
        at = slice(tile * LANES, (tile + 1) * LANES)
        old = prior * cent_ref[:, at].astype(jnp.float32)
        nc = (totals[:, at] + old) * inv[...]
        nc_v[:, at] = nc
        table[pl.ds(tile, lists, stride=tiles), :] = nc
    nc_copy = pltpu.make_async_copy(nc_v, nc_ref, nc_sem)
    nc_copy.start()
    copy.wait()

    def pick(q, _):
        for u in range(8):
            r = q * 8 + u
            row = table[pl.ds(pl.multiple_of(ids_s[0, r], 8), tiles), :]
            picked[pl.ds(pl.multiple_of(r * tiles, 8), tiles), :] = row
        return 0

    lax.fori_loop(0, rows // 8, pick, 0, unroll=8)

    def residuals(j, _):
        at = pl.ds(pl.multiple_of(j * COLS, COLS), COLS)
        line = lax.broadcasted_iota(jnp.int32, (LANES, COLS), 0)
        column = lax.broadcasted_iota(jnp.int32, (LANES, COLS), 1)
        widen = jnp.where(line == j * here + column // width, 1.0, 0.0).astype(jnp.bfloat16)
        line = lax.broadcasted_iota(jnp.int32, (COLS, LANES), 0)
        column = lax.broadcasted_iota(jnp.int32, (COLS, LANES), 1)
        fold = jnp.where(
            lax.rem(column, subs) == j * here + line // width, 1.0, 0.0
        ).astype(jnp.bfloat16)
        for i in range(rows // chunk):
            ra = slice(i * chunk, (i + 1) * chunk)
            near = jnp.concatenate(
                [
                    picked[pl.ds(i * chunk * tiles + j * side + h, chunk, stride=tiles), :]
                    for h in range(side)
                ],
                axis=1,
            )
            r = (arr_ref[ra, at].astype(jnp.float32) - near).astype(jnp.bfloat16)
            wide = r.astype(jnp.float32)
            low = r * dot(side_v[ra, 3 * LANES :], widen).astype(jnp.bfloat16)
            low_v[ra, at] = low
            high_v[ra, at] = r - low
            square = wide * wide
            square_hi = square.astype(jnp.bfloat16)
            square_lo = (square - square_hi.astype(jnp.float32)).astype(jnp.bfloat16)
            found = dot(square_hi, fold) + dot(square_lo, fold)
            norms[ra, :] = jnp.where(j == 0, found, norms[ra, :] + found)
        return 0

    lax.fori_loop(0, dims // COLS, residuals, 0, unroll=2)

    for i in range(rows // chunk):
        ra = slice(i * chunk, (i + 1) * chunk)
        pieces = split3(norms[ra, :] * side_v[ra, 3 * LANES :].astype(jnp.float32))
        for k, piece in enumerate(pieces):
            side_v[ra, k * LANES : (k + 1) * LANES] = piece

    def columns(j, _):
        line = lax.broadcasted_iota(jnp.int32, (kinds * LANES, COLS), 0)
        column = lax.broadcasted_iota(jnp.int32, (kinds * LANES, COLS), 1)
        spot = lax.rem(column, LANES // 2)
        in_first = lax.rem(column, LANES) >= LANES // 2
        kind = spot // (2 * quad)
        half = lax.rem(spot, 2 * quad) // quad
        sub = (
            j * here
            + (column // LANES) * group
            + jnp.where(in_first, 0, quad)
            + lax.rem(spot, quad)
        )
        wanted = kind * LANES + half * subs + sub
        move = jnp.where((line == wanted) & (kind < kinds), 1.0, 0.0).astype(jnp.bfloat16)
        for i in range(2 * rows // chunk):
            ra = slice(i * chunk // 2, (i + 1) * chunk // 2)
            extra[ra, :] = dot(side_v[ra, :], move).astype(jnp.bfloat16)

        level = lax.broadcasted_iota(jnp.int32, (LANES, rows), 0)
        level = level.astype(jnp.float32).astype(jnp.bfloat16)
        one = jnp.ones((), jnp.bfloat16)
        zero = jnp.zeros((), jnp.bfloat16)
        lane = lax.broadcasted_iota(jnp.int32, (LANES, LANES), 1)
        wide_lane = lax.broadcasted_iota(jnp.int32, (rows, LANES), 1)
        steps = subs // parts // here
        for part in range(side):
            at = pl.ds(pl.multiple_of(j * COLS + part * LANES, LANES), LANES)
            codes = code_t[j * side + part].astype(jnp.float32).astype(jnp.bfloat16)
            beside = extra[:, part * LANES : (part + 1) * LANES]
            low_sum = jnp.zeros((LANES, LANES), jnp.float32)
            high_sum = low_sum
            extra_sum = low_sum
            for q in range(2):
                own = (wide_lane < LANES // 2) == (q == 0)
                mixed = jnp.where(own, high_v[:, at], beside)
                weights = jnp.concatenate([low_v[:, at], mixed], axis=1)
                apart = (lane >= LANES // 2) == (q == 0)
                onehot = jnp.concatenate(
                    [
                        jnp.where(level == codes[i : i + 1], one, zero)
                        for i in range(q * quad, (q + 1) * quad)
                    ],
                    axis=0,
                )
                every = dot(onehot, weights)
                for k in range(quad):
                    i = q * quad + k
                    found = every[k * LANES : (k + 1) * LANES]
                    low_sum = jnp.where(lane // width == i, found[:, :LANES], low_sum)
                    high_sum = jnp.where(lane // width == i, found[:, LANES:], high_sum)
                    extra_sum = jnp.where(
                        apart & (lax.rem(lane, quad) == k), found[:, LANES:], extra_sum
                    )
            low_t = jnp.transpose(low_sum)
            high_t = jnp.transpose(high_sum)
            extra_t = jnp.transpose(extra_sum)
            for i in range(group):
                q, k = divmod(i, quad)
                base = LANES // 2 if q == 0 else 0
                blocks = []
                for half, sums in ((0, low_t), (1, high_t)):
                    found = [
                        extra_t[row : row + 1]
                        for row in range(base + half * quad + k, base + LANES // 2, 2 * quad)
                    ]
                    norm = (found[0] + found[1]) + found[2]
                    blocks.append(
                        jnp.concatenate(
                            [sums[i * width : (i + 1) * width], found[3], norm], axis=0
                        )
                    )
                sub = (j % steps) * here + part * group + i
                near = subs // parts // FAR
                at_row = ((j // steps * near + sub % near) * FAR + sub // near) * held
                keep_ref[pl.ds(at_row, held), :] = jnp.where(first_core, blocks[0], blocks[1])
                give_ref[pl.ds(at_row, held), :] = jnp.where(first_core, blocks[1], blocks[0])
        return 0

    for j in range(dims // COLS):
        columns(j, 0)
    nc_copy.wait()


def local_pass(core, arrived, centroids, subs, width, prior, parts):
    rows = arrived.shape[0]
    lists, dims = centroids.shape
    tiles = dims // LANES
    group = LANES // width
    sums = jax.ShapeDtypeStruct((subs * (width + 2), LANES), jnp.float32)
    return pl.pallas_call(
        functools.partial(local_kernel, subs, width, parts, prior, 256),
        in_specs=[pl.BlockSpec(memory_space=pltpu.SMEM), IN_VMEM, IN_VMEM],
        out_specs=[pl.BlockSpec(memory_space=pl.ANY), IN_VMEM, IN_VMEM],
        out_shape=[jax.ShapeDtypeStruct((lists, dims), jnp.float32), sums, sums],
        scratch_shapes=[
            pltpu.VMEM((lists, rows), jnp.bfloat16),
            pltpu.VMEM((lists, LANES), jnp.float32),
            pltpu.VMEM((subs // group, group, rows), jnp.int32),
            pltpu.VMEM((lists * tiles, LANES), jnp.float32),
            pltpu.VMEM((rows * tiles, LANES), jnp.float32),
            pltpu.VMEM((rows, dims), jnp.bfloat16),
            pltpu.VMEM((rows, dims), jnp.bfloat16),
            pltpu.VMEM((rows, LANES), jnp.float32),
            pltpu.VMEM((rows, 4 * LANES), jnp.bfloat16),
            pltpu.VMEM((rows, COLS), jnp.bfloat16),
            pltpu.VMEM((1, rows), jnp.int32),
            pltpu.SMEM((1, rows), jnp.int32),
            pltpu.VMEM((lists, dims), jnp.float32),
            pltpu.SemaphoreType.DMA,
            pltpu.SemaphoreType.DMA,
        ],
        compiler_params=pltpu.CompilerParams(vmem_limit_bytes=32 * MIB),
        name="local_pass",
    )(core, arrived, centroids)


def owner_kernel(width, prior, copies, part_ref, old_ref, out_ref):
    held = width + 2
    sources = part_ref.shape[0] // held
    taken = [part_ref[pl.ds(i, sources, stride=held), :] for i in range(held)]
    sums, counts, norms = taken[:width], taken[width], taken[width + 1]
    count = jnp.sum(counts, axis=0, keepdims=True)
    share = 1.0 / jnp.maximum(counts, 1.0)
    inner = norms
    outer = jnp.zeros_like(norms)
    rows = []
    for d in range(width):
        total = jnp.sum(sums[d], axis=0, keepdims=True)
        new = (total + prior * old_ref[d : d + 1]) / (count + prior)
        mean = sums[d] * share
        gap = mean - new
        inner = inner - sums[d] * mean
        outer = outer + gap * gap
        rows.append(new)
    errors = jnp.sum(jnp.maximum(inner, 0.0) + counts * outer, axis=0, keepdims=True)
    rows.append(errors / (count + 1.0))
    result = jnp.concatenate(rows, axis=0)
    for c in range(copies):
        out_ref[c * (width + 1) : (c + 1) * (width + 1)] = result


def half_kernel(width, flip, core_ref, part_ref, *refs):
    table_ref, dist_ref, table_v, dist_v, sems = refs[-5:]
    held = width + 1
    subs = table_ref.shape[0]
    half = core_ref[0] if flip == 0 else 1 - core_ref[0]
    at = pl.ds(pl.multiple_of(half * LANES, LANES), LANES)
    dist_v[...] = part_ref[pl.ds(width, subs, stride=held), :]
    dist_move = pltpu.make_async_copy(dist_v, dist_ref.at[:, at], sems.at[0])
    dist_move.start()
    for m in range(subs):
        table_v[m] = part_ref[m * held : m * held + width]
    table_move = pltpu.make_async_copy(table_v, table_ref.at[:, :, at], sems.at[1])
    table_move.start()
    dist_move.wait()
    table_move.wait()


def write_half(flip, core, part, shapes, held_before):
    subs, width, _ = shapes[0].shape
    anywhere = pl.BlockSpec(memory_space=pl.ANY)
    return pl.pallas_call(
        functools.partial(half_kernel, width, flip),
        in_specs=[pl.BlockSpec(memory_space=pltpu.SMEM), IN_VMEM]
        + [anywhere] * len(held_before),
        out_specs=[anywhere, anywhere],
        out_shape=list(shapes),
        input_output_aliases={2: 0, 3: 1} if held_before else {},
        scratch_shapes=[
            pltpu.VMEM((subs, width, LANES), jnp.float32),
            pltpu.VMEM((subs, LANES), jnp.float32),
            pltpu.SemaphoreType.DMA((2,)),
        ],
        compiler_params=pltpu.CompilerParams(vmem_limit_bytes=8 * MIB),
        cost_estimate=pl.CostEstimate(flops=0, bytes_accessed=4 * MIB, transcendentals=0),
        name="own_half" if flip == 0 else "other_half",
    )(core, part, *held_before)


def on_device(vectors, list_ids, codes, centroids, codebooks):
    rows, dims = vectors.shape
    chips = lax.axis_size("far") * lax.axis_size("plane")
    parts = lax.axis_size("sub")
    owners = chips * CORES * parts
    lists = centroids.shape[0]
    subs = codes.shape[1]
    my_subs, width, levels = codebooks.shape
    prior_lists = float(rows // lists)
    prior_codes = float(rows * owners // levels)
    core = lax.axis_index("core")
    core_arg = core.astype(jnp.int32).reshape(1)
    swap = [(0, 1), (1, 0)]

    place = jnp.stack([lax.axis_index(CHIP), core]).astype(jnp.int32)
    run = rows // (chips * CORES)
    sent, old = pack(place, vectors, list_ids, codes, codebooks, lists, run)
    arrived = lax.all_to_all(sent, ROW_ORDER, split_axis=0, concat_axis=0, tiled=True)
    new_centroids, keep, give = local_pass(
        core_arg, arrived, centroids, subs, width, prior_lists, parts
    )
    paired = keep + lax.ppermute(give, "core", swap)
    held = width + 2
    mine = lax.all_to_all(
        paired.reshape(chips * parts, 1, held * LANES),
        SUM_ORDER,
        split_axis=0,
        concat_axis=0,
        tiled=True,
    ).reshape(chips * parts * held, LANES)
    held = width + 1
    done = pl.pallas_call(
        functools.partial(owner_kernel, width, prior_codes, chips),
        in_specs=[IN_VMEM, IN_VMEM],
        out_specs=IN_VMEM,
        out_shape=jax.ShapeDtypeStruct((chips * held, LANES), jnp.float32),
        compiler_params=pltpu.CompilerParams(vmem_limit_bytes=8 * MIB),
        name="owner_pass",
    )(mine, old)
    half = lax.all_to_all(
        done.reshape(chips, 1, held * LANES), CHIP, split_axis=0, concat_axis=0, tiled=True
    ).reshape(chips * held, LANES)
    other = lax.ppermute(half, "core", swap)
    shapes = (
        jax.ShapeDtypeStruct((my_subs, width, levels), jnp.float32),
        jax.ShapeDtypeStruct((my_subs, levels), jnp.float32),
    )
    first = write_half(0, core_arg, half, shapes, ())
    table, distortion = write_half(1, core_arg, other, shapes, tuple(first))
    return new_centroids, table, distortion


def solution(mesh):
    parts = mesh.shape["sub"]
    cores = Mesh(mesh.devices.reshape(FAR, -1, CORES, parts), SPLIT)
    in_specs = (
        P(SPLIT, None),
        P(SPLIT),
        P(SPLIT, None),
        P(SPLIT, None),
        P("sub", None, None),
    )
    out_specs = (P(SPLIT, None), P("sub", None, None), P("sub", None))
    return jax.shard_map(
        on_device, mesh=cores, in_specs=in_specs, out_specs=out_specs, check_vma=False
    )
```
